32 devices in a mesh: twin: 2 (over y), gx: 4 (over z), gy: 2 (over core), gz: 2 (over x).
Axes of the slice: x: 2, y: 2, z: 4, core: 2. Of those that a mesh axis runs over, the one named last changes fastest.
Arguments:
- potential: float32 [64, 32, 256], P(('twin', 'gx'), 'gy', 'gz'), parts along dimension 0, may hold values from 0 to 1
- gating: float32 [64, 32, 256], P(('twin', 'gx'), 'gy', 'gz'), parts along dimension 0, may hold values from 0 to 1
- adjoint_v: float32 [64, 32, 256], P(('twin', 'gx'), 'gy', 'gz'), parts along dimension 0, may hold values from -6 to 6
- adjoint_h: float32 [64, 32, 256], P(('twin', 'gx'), 'gy', 'gz'), parts along dimension 0, may hold values from -6 to 6
- recorded: float32 [64, 32, 256], P(('twin', 'gx'), 'gy', 'gz'), parts along dimension 0, may hold values from 0 to 1
- tissue_mask: int32 [64, 32, 256], P(('twin', 'gx'), 'gy', 'gz'), parts along dimension 0, may hold values from 0 to 1
- fibre_sector: int32 [64, 32, 256], P(('twin', 'gx'), 'gy', 'gz'), parts along dimension 0, may hold values from 0 to 11
- region_label: int32 [64, 32, 256], P(('twin', 'gx'), 'gy', 'gz'), parts along dimension 0, may hold values from 0 to 15
- fibre_table: float32 [24, 9], P('twin'), parts along dimension 0, may hold values from 0.005 to 0.025
- conductance: float32 [32], P('twin'), parts along dimension 0, may hold values from 0.5 to 2
Outputs:
- lambda_v: float32 [64, 32, 256], P(('twin', 'gx'), 'gy', 'gz'), parts along dimension 0
- lambda_h: float32 [64, 32, 256], P(('twin', 'gx'), 'gy', 'gz'), parts along dimension 0
- sensitivity: float32 [32], P('twin'), parts along dimension 0
The draws below stay inside these ranges and needn't reach their ends.
There are 2 independent parts, one for each index of `twin`. The reference program is written for one: setup_inputs(seed, part) draws one part's arguments, and reference() takes and returns one part's arrays. A program takes and returns all parts, laid end to end along the dimension named above; each array names one. Nothing has to cross between parts.
All inputs are finite; a program needn't handle non-finite values.
Results may differ from the reference program's by a relative error of at most 0.0003.
Values sent between devices are 32-bit elements; how exact they have to be, the bound alone decides.
A program may use at most 64 MiB of HBM per device.

```python
import math
import jax
import jax.numpy as jnp

WINDOW_STEPS = 3
SECTORS = 12
REGIONS = 16
NX = 32
NY = 32
NZ = 256


def draw_tissue_mask(key, part):
    local = jax.random.fold_in(key, 17)
    xs = jnp.arange(NX, dtype=jnp.int32)[:, None, None]
    ys = jnp.arange(NY, dtype=jnp.int32)[None, :, None]
    zs = jnp.arange(NZ, dtype=jnp.int32)[None, None, :]
    coord_x = (2 * xs + 1 - NX) * 1000 // NX
    coord_y = (2 * ys + 1 - NY) * 1000 // NY
    coord_z = (2 * zs + 1 - NZ) * 1000 // NZ
    radial = coord_y * coord_y + coord_z * coord_z
    outer = coord_x * coord_x + radial < 950 * 950
    cavity_left = (coord_x + 300) * (coord_x + 300) + radial < 450 * 450
    cavity_right = (coord_x - 350) * (coord_x - 350) + radial < 330 * 330
    holes = jax.random.randint(local, (NX, NY, NZ), 0, 10) > 0
    inside = outer & jnp.logical_not(cavity_left) & jnp.logical_not(cavity_right) & holes
    return jnp.where(inside, 1, 0).astype(jnp.int32)


def draw_region_label(key, part):
    local = jax.random.fold_in(key, 29)
    xs = jnp.arange(NX, dtype=jnp.int32)[:, None, None]
    slab = xs * (REGIONS // 2) // NX
    extra = jax.random.randint(local, (NX, NY, NZ), 0, 2)
    return (slab * 2 + extra).astype(jnp.int32)


def place_ends(drawn, own_key, smallest, top_value):
    longest = drawn.shape.index(max(drawn.shape))
    spots = []
    for shift in (0, 1):
        where = [jax.random.randint(jax.random.fold_in(own_key, axis), (), 0, length) for axis, length in enumerate(drawn.shape)]
        where[longest] = (where[longest] + shift) % drawn.shape[longest]
        spots.append(tuple(where))
    return drawn.at[spots[0]].set(smallest).at[spots[1]].set(top_value)


def block_scale(own_key, dims, pieces, low, largest):
    def one(axis_at, blocks):
        heights = jax.random.uniform(jax.random.fold_in(jax.random.fold_in(own_key, 6), axis_at), (blocks,), jnp.float32, low / len(pieces), largest / len(pieces))
        return jnp.repeat(jnp.exp(heights), dims[axis_at] // blocks).reshape((-1,) + (1,) * (len(dims) - axis_at - 1))

    gain = one(*pieces[0])
    for cut in pieces[1:]:
        gain = gain * one(*cut)
    return gain


def noise(stream_key, shape, deviation, most, shards=(), kind=jnp.bfloat16):
    result = deviation * jax.random.normal(stream_key, shape, jnp.float32)
    if shards:
        result = result * block_scale(stream_key, shape, shards, -0.22, 0.18)
    return jnp.clip(result, -most, most).astype(kind)


def setup_inputs(seed: int = 0, part: int = 0) -> dict:
    keys = jax.random.split(jax.random.key(seed), 11)
    own_keys = jax.random.split(jax.random.fold_in(keys[10], part), 11)
    return {
        "potential": jnp.clip(1.0 * jax.random.uniform(own_keys[0], (NX, NY, NZ), jnp.float32) ** block_scale(own_keys[0], (NX, NY, NZ), ((0, 4), (1, 2), (2, 2)), -0.2, 0.2), 0.0, 1.0),
        "gating": jnp.clip(1.0 * jax.random.uniform(own_keys[1], (NX, NY, NZ), jnp.float32) ** block_scale(own_keys[1], (NX, NY, NZ), ((0, 4), (1, 2), (2, 2)), -0.2, 0.2), 0.0, 1.0),
        "adjoint_v": noise(own_keys[2], (NX, NY, NZ), 1.0, 6.0, ((0, 4), (1, 2), (2, 2)), jnp.float32),
        "adjoint_h": noise(own_keys[3], (NX, NY, NZ), 1.0, 6.0, ((0, 4), (1, 2), (2, 2)), jnp.float32),
        "recorded": jnp.clip(1.0 * jax.random.uniform(own_keys[4], (NX, NY, NZ), jnp.float32) ** block_scale(own_keys[4], (NX, NY, NZ), ((0, 4), (1, 2), (2, 2)), -0.2, 0.2), 0.0, 1.0),
        "tissue_mask": draw_tissue_mask(jax.random.fold_in(jax.random.fold_in(keys[10], part), 71), part),
        "fibre_sector": place_ends(jax.random.randint(own_keys[6], (NX, NY, NZ), 0, SECTORS), jax.random.fold_in(own_keys[6], 1), 0, SECTORS - 1).astype(jnp.int32),
        "region_label": draw_region_label(jax.random.fold_in(jax.random.fold_in(keys[10], part), 71), part),
        "fibre_table": jnp.clip(jnp.exp(jax.random.uniform(own_keys[8], (SECTORS, 9), jnp.float32, math.log(0.005), math.log(0.025))), 0.005, 0.025),
        "conductance": jnp.clip(jnp.exp(jax.random.uniform(own_keys[9], (REGIONS,), jnp.float32, math.log(0.5), math.log(2.0))), 0.5, 2.0),
    }


step_size = 0.1
tau_inward = 0.3
tau_outward = 6.0
tau_opening = 12.0
tau_closing = 15.0
gate_level = 0.13
gate_width = 0.02
gradient_gain = 30.0
PAIR_OFFSETS = ((1, 0, 0), (0, 1, 0), (0, 0, 1), (1, 1, 0), (1, -1, 0), (1, 0, 1), (1, 0, -1), (0, 1, 1), (0, 1, -1))

def crop(array, trim):
    if trim == 0:
        return array
    return array[..., trim:-trim, trim:-trim, trim:-trim]

def shifted(padded, offset):
    sizes = [padded.shape[-3 + axis] - 2 for axis in range(3)]
    starts = [1 + offset[axis] for axis in range(3)]
    return padded[..., starts[0]:starts[0] + sizes[0], starts[1]:starts[1] + sizes[1], starts[2]:starts[2] + sizes[2]]

def neighbour_terms(field_pad, tissue_pad, flux_pad):
    centre = crop(field_pad, 1)
    tissue_mid = crop(tissue_pad, 1)
    flux_mid = crop(flux_pad, 1)
    total = jnp.zeros_like(centre)
    for direction, base in enumerate(PAIR_OFFSETS):
        for sign in (1, -1):
            offset = tuple((sign * part for part in base))
            coupling = 0.5 * (flux_mid[direction] * shifted(tissue_pad, offset) + shifted(flux_pad[direction], offset) * tissue_mid)
            total = total + coupling * (shifted(field_pad, offset) - centre)
    return total

def region_terms(adjoint_pad, field_pad, tissue_pad, fibre_mid):
    adjoint_mid = crop(adjoint_pad, 1)
    centre = crop(field_pad, 1)
    total = jnp.zeros_like(centre)
    for direction, base in enumerate(PAIR_OFFSETS):
        for sign in (1, -1):
            offset = tuple((sign * part for part in base))
            weight = shifted(tissue_pad, offset) * fibre_mid[direction]
            total = total + weight * (shifted(adjoint_pad, offset) - adjoint_mid) * (shifted(field_pad, offset) - centre)
    return -0.5 * crop(tissue_pad, 1) * total

def ionic(volts, gate_now):
    switch = jax.nn.sigmoid((volts - gate_level) / gate_width)
    drive_v = gate_now * volts * volts * (1.0 - volts) / tau_inward - volts / tau_outward
    drive_h = (1.0 - switch) * (1.0 - gate_now) / tau_opening - switch * gate_now / tau_closing
    return (drive_v, drive_h)

def ionic_partials(volts, gate_now):
    switch = jax.nn.sigmoid((volts - gate_level) / gate_width)
    slope = switch * (1.0 - switch) / gate_width
    deriv_vv = gate_now * (2.0 * volts - 3.0 * volts * volts) / tau_inward - 1.0 / tau_outward
    deriv_vh = volts * volts * (1.0 - volts) / tau_inward
    deriv_hv = slope * (-(1.0 - gate_now) / tau_opening - gate_now / tau_closing)
    deriv_hh = -(1.0 - switch) / tau_opening - switch / tau_closing
    return (deriv_vv, deriv_vh, deriv_hv, deriv_hh)

def forward_step(volts_pad, gate_now, tissue_mid, tissue_pad, flux_pad):
    volts = crop(volts_pad, 1)
    drive_v, drive_h = ionic(volts, gate_now)
    spread = neighbour_terms(volts_pad, tissue_pad, flux_pad)
    return (volts + tissue_mid * (spread + step_size * drive_v), gate_now + tissue_mid * step_size * drive_h)

def reference(potential, gating, adjoint_v, adjoint_h, recorded, tissue_mask, fibre_sector, region_label, fibre_table, conductance):
    fields = jnp.stack([tissue_mask, fibre_sector, region_label])
    fields_pad = jnp.pad(fields, ((0, 0), (1, 1), (1, 1), (1, 1)))
    tissue_pad = fields_pad[0].astype(jnp.float32)
    fibre_pad = jnp.moveaxis(fibre_table[fields_pad[1]], -1, 0)
    flux_pad = (tissue_pad * conductance[fields_pad[2]])[None] * fibre_pad
    tissue_mid = crop(tissue_pad, 1)
    fibre_mid = crop(fibre_pad, 1)
    volts, gate_now = (potential, gating)
    saved_pads = []
    saved_gates = []
    for step in range(WINDOW_STEPS):
        volts_pad = jnp.pad(volts, 1)
        saved_pads.append(volts_pad)
        saved_gates.append(gate_now)
        volts, gate_now = forward_step(volts_pad, gate_now, tissue_mid, tissue_pad, flux_pad)
    back_v = adjoint_v + tissue_mid * (volts - recorded)
    back_h = adjoint_h
    total = jnp.zeros((REGIONS,), jnp.float32)
    for step in reversed(range(WINDOW_STEPS)):
        masked = tissue_mid * back_v
        masked_pad = jnp.pad(masked, 1)
        volts_pad = saved_pads[step]
        terms = region_terms(masked_pad, volts_pad, tissue_pad, fibre_mid)
        total = total + jax.ops.segment_sum(terms.ravel(), region_label.ravel(), num_segments=REGIONS)
        deriv_vv, deriv_vh, deriv_hv, deriv_hh = ionic_partials(crop(volts_pad, 1), saved_gates[step])
        spread = neighbour_terms(masked_pad, tissue_pad, flux_pad)
        next_v = back_v + spread + step_size * tissue_mid * (deriv_vv * back_v + deriv_hv * back_h)
        next_h = back_h + step_size * tissue_mid * (deriv_vh * back_v + deriv_hh * back_h)
        back_v, back_h = (next_v, next_h)
    scale = gradient_gain / math.sqrt(NX * NY * NZ / REGIONS)
    return (back_v, back_h, total * scale)
```

```python
import functools
import math

import jax
import jax.numpy as jnp
from jax import lax
from jax.experimental import pallas as pl
from jax.experimental.pallas import tpu as pltpu
from jax.sharding import PartitionSpec as P

WINDOW_STEPS = 3

step_size = 0.1
tau_inward = 0.3
tau_outward = 6.0
tau_opening = 12.0
tau_closing = 15.0
gate_level = 0.13
gate_width = 0.02
gradient_gain = 30.0
PAIR_OFFSETS = (
    (1, 0, 0),
    (0, 1, 0),
    (0, 0, 1),
    (1, 1, 0),
    (1, -1, 0),
    (1, 0, 1),
    (1, 0, -1),
    (0, 1, 1),
    (0, 1, -1),
)
OFFSETS = tuple(
    (d, tuple(sign * part for part in base))
    for d, base in enumerate(PAIR_OFFSETS)
    for sign in (1, -1)
)
VARIANTS = tuple((dy, dz) for dy in (0, 1, -1) for dz in (0, 1, -1))
FLIP = 2
MESH = pl.DeviceIdType.MESH


def moves(size):
    if size == 1:
        return ()
    return (FLIP,) if size == 2 else (1, -1)


def messages(ny, nz):
    found = []
    for mx in (0, 1, -1):
        for my in (0,) + moves(ny):
            for mz in (0,) + moves(nz):
                if 1 <= (mx != 0) + (my != 0) + (mz != 0) <= 2:
                    found.append((mx, my, mz))
    return found


def land_shape(move, fields, shape):
    lx, ly, lz = shape
    mx, my, mz = move
    if mz:
        return (fields, 8 if my else ly, lz)
    return (fields, 1 if mx else lx, 8 if my else ly, lz)


def kernel(
    counts,
    phase_fields,
    regions,
    sectors,
    scale,
    table_ref,
    cond_ref,
    v_ref,
    h_ref,
    av_ref,
    ah_ref,
    rec_ref,
    tissue_ref,
    sector_ref,
    region_ref,
    out_v,
    out_h,
    out_s,
    coef,
    grad,
    diag,
    vvar,
    mvar,
    partial,
    gathered,
    red_send,
    red_recv,
    *rest,
):
    nx, ny, nz = counts
    shape = v_ref.shape
    lx, ly, lz = shape
    moved = messages(ny, nz)
    rest = list(rest)
    phases = []
    for _ in phase_fields:
        stage = [rest.pop(0) for _ in range(4)]
        land = {move: rest.pop(0) for move in moved}
        phases.append((stage, land, rest.pop(0), rest.pop(0)))

    ix, iy, iz = lax.axis_index("gx"), lax.axis_index("gy"), lax.axis_index("gz")
    n = nx * ny * nz
    me = (ix * ny + iy) * nz + iz

    def device(index):
        return {"gx": index // (ny * nz), "gy": (index // nz) % ny, "gz": index % nz}

    barrier = pltpu.get_barrier_semaphore()

    def greet(rel, carry):
        pl.semaphore_signal(
            barrier, inc=1, device_id=device((me + rel) % n), device_id_type=MESH
        )
        return carry

    def each_other(body):
        if n <= 64:
            for rel in range(1, n):
                body(rel, 0)
        else:
            lax.fori_loop(1, n, body, 0)

    each_other(greet)

    def along(index, count, move):
        if move == 0:
            return index, None
        if move == FLIP:
            return 1 - index, None
        return index + move, (index < count - 1) if move == 1 else (index > 0)

    def both(conds):
        conds = [c for c in conds if c is not None]
        if not conds:
            return None
        out = conds[0]
        for c in conds[1:]:
            out = jnp.logical_and(out, c)
        return out

    def guarded(cond, body):
        if cond is None:
            body()
        else:
            pl.when(cond)(body)

    def copy_of(phase, k):
        (sx, sy, sz, syz), land, send, recv = phases[phase]
        mx, my, mz = move = moved[k]
        tx, cx = along(ix, nx, mx)
        ty, cy = along(iy, ny, my)
        tz, cz = along(iz, nz, mz)
        back = [along(i, c, m if m == FLIP else -m)[1] for i, c, m in
                ((ix, nx, mx), (iy, ny, my), (iz, nz, mz))]
        if mz:
            src = syz if my else sz
        elif my:
            src = sy
            if mx:
                src = sy.at[:, pl.ds(lx - 1 if mx == 1 else 0, 1)]
        else:
            src = sx.at[:, pl.ds(1 if mx == 1 else 0, 1)]
        copy = pltpu.make_async_remote_copy(
            src_ref=src,
            dst_ref=land[move],
            send_sem=send.at[k],
            recv_sem=recv.at[k],
            device_id={"gx": tx, "gy": ty, "gz": tz},
            device_id_type=MESH,
        )
        return copy, both((cx, cy, cz)), both(back)

    lane3 = lax.broadcasted_iota(jnp.int32, (1, 1, lz), 2)
    sub8 = lax.broadcasted_iota(jnp.int32, (8, lz), 0)
    lane = lax.broadcasted_iota(jnp.int32, (ly, lz), 1)
    lane8 = lax.broadcasted_iota(jnp.int32, (8, lz), 1)

    def roll(x, shift, axis):
        size = x.shape[axis]
        shift = shift % size
        return x if shift == 0 else pltpu.roll(x, shift, axis)

    def stage_fields(phase, fields):
        sx, sy, sz, syz = phases[phase][0]
        for f, u in enumerate(fields):
            sx[f, 0] = u[0]
            sx[f, 1] = u[lx - 1]
            sy[f] = jnp.where((sub8 < 4)[None], u[:, :8], u[:, ly - 8 :])
            packed = jnp.zeros((ly, lz), jnp.float32)
            for p in range(lx):
                edge = jnp.where(lane == 0, roll(u[p], 1, 1), roll(u[p], -1, 1))
                here = (lane == 2 * p) | (lane == 2 * p + 1)
                packed = jnp.where(here, roll(edge, 2 * p + 1, 1), packed)
            sz[f] = packed
            syz[f] = jnp.where(sub8 < 4, packed[:8], packed[ly - 8 :])

    def send(phase):
        for k in range(len(moved)):
            copy, cond, _ = copy_of(phase, k)
            guarded(cond, copy.start)

    def receive(phase):
        for k in range(len(moved)):
            copy, _, cond = copy_of(phase, k)
            guarded(cond, copy.wait_recv)

    def finish_sends(phase):
        for k in range(len(moved)):
            copy, cond, _ = copy_of(phase, k)
            guarded(cond, copy.wait_send)

    one = lambda cond: jnp.where(cond, 1, 0)
    has_x = {1: one(ix > 0), -1: one(ix < nx - 1)}
    yp, ym, zp, zm = one(iy < ny - 1), one(iy > 0), one(iz < nz - 1), one(iz > 0)

    def fetch(phase, f, mx, in_y, in_z):
        land = phases[phase][1]
        rows, lanes = (sub8, lane8) if in_y else (None, lane)
        if in_y:
            y_parts = [
                (m, jnp.where(sub8 < 4, yp if m != 1 else 0, ym if m != -1 else 0))
                for m in moves(ny)
            ]
        else:
            y_parts = [(0, None)]
        if in_z:
            z_parts = [
                (m, jnp.where(lanes % 2 == 0, zp if m != 1 else 0, zm if m != -1 else 0))
                for m in moves(nz)
            ]
        else:
            z_parts = [(0, None)]
        out = None
        for my, cy in y_parts:
            for mz, cz in z_parts:
                value = land[(mx, my, mz)][f]
                ok = has_x[mx] if mx else 1
                for c in (cy, cz):
                    if c is not None:
                        ok = c * ok
                keep = jnp.broadcast_to(ok, value.shape[-2:]) > 0
                if value.ndim == 3:
                    keep = keep[None]
                other = jnp.zeros_like(value) if out is None else out
                out = jnp.where(jnp.broadcast_to(keep, value.shape), value, other)
        return out

    def halo(phase, f):
        return dict(
            x={m: fetch(phase, f, m, False, False)[0] for m in (1, -1)},
            y=fetch(phase, f, 0, True, False),
            xy={m: fetch(phase, f, m, True, False)[0] for m in (1, -1)},
            z=fetch(phase, f, 0, False, True),
            xz={m: fetch(phase, f, m, False, True) for m in (1, -1)},
            yz=fetch(phase, f, 0, True, True),
        )

    def extend(u, parts):
        middle = jnp.concatenate([u, parts["y"]], axis=1)
        ends = {m: jnp.concatenate([parts["x"][m], parts["xy"][m]], axis=0) for m in (1, -1)}
        planes = [ends[1]] + [middle[p] for p in range(lx)] + [ends[-1]]
        z_rows = jnp.concatenate([parts["z"], parts["yz"]], axis=0)
        edges = (
            [roll(parts["xz"][1], -(2 * lx - 1), 1)]
            + [roll(z_rows, -(2 * p + 1), 1) for p in range(lx)]
            + [roll(parts["xz"][-1], -1, 1)]
        )
        return planes, edges

    def variant(ext, dy, dz, p):
        planes, edges = ext
        x = planes[p]
        outer = p in (0, lx + 1)
        if outer and dy and dz:
            return None
        if dz:
            rows = ly if dy == 0 else ly + 8
            at = lax.broadcasted_iota(jnp.int32, (rows, lz), 1)
            x = jnp.where(
                at == (lz - 1 if dz == 1 else 0), edges[p][:rows], roll(x[:rows], -dz, 1)
            )
        if dy:
            x = roll(x, -dy, 0)
        return x[:ly]

    def store_variants(ref, where, ext):
        for k, (dy, dz) in enumerate(VARIANTS):
            for p in range(lx + 2):
                x = variant(ext, dy, dz, p)
                if x is not None:
                    ref[where, k, p] = x

    def neighbour(ref, where, offset, p):
        return ref[where, VARIANTS.index(offset[1:]), p + 1 + offset[0]]

    tissue = tissue_ref[...].astype(jnp.float32)
    factor = jnp.zeros(shape, jnp.float32)
    for label in range(regions):
        factor = jnp.where(region_ref[...] == label, cond_ref[label], factor)
    factor = tissue * factor
    sector = sector_ref[...].astype(jnp.float32)
    stage_fields(0, (factor, sector, v_ref[...]))
    pl.semaphore_wait(barrier, n - 1)
    send(0)

    def fibres(codes):
        found = [jnp.zeros(codes.shape, jnp.float32) for _ in PAIR_OFFSETS]
        for label in range(sectors):
            same = codes == float(label)
            for d in range(len(PAIR_OFFSETS)):
                found[d] = jnp.where(same, table_ref[label, d], found[d])
        return found

    def ionic(volts, gate):
        s = 1.0 / (1.0 + jnp.exp(-(volts - gate_level) / gate_width))
        drive_v = gate * volts * volts * (1.0 - volts) / tau_inward - volts / tau_outward
        drive_h = (1.0 - s) * (1.0 - gate) / tau_opening - s * gate / tau_closing
        return drive_v, drive_h

    def partials(volts, gate):
        s = 1.0 / (1.0 + jnp.exp(-(volts - gate_level) / gate_width))
        slope = s * (1.0 - s) / gate_width
        vv = gate * (2.0 * volts - 3.0 * volts * volts) / tau_inward - 1.0 / tau_outward
        vh = volts * volts * (1.0 - volts) / tau_inward
        hv = slope * (-(1.0 - gate) / tau_opening - gate / tau_closing)
        hh = -(1.0 - s) / tau_opening - s / tau_closing
        return vv, vh, hv, hh

    def spread(ref, where, u, p):
        total = -diag[p] * u
        for o, (_, offset) in enumerate(OFFSETS):
            total = total + coef[o, p] * neighbour(ref, where, offset, p)
        return total

    fibre = fibres(sector)
    flux = [factor * f for f in fibre]
    volts, gate = v_ref[...], h_ref[...]
    drive_v, drive_h = ionic(volts, gate)

    receive(0)
    fac_halo = halo(0, 0)
    sec_halo = halo(0, 1)
    fac_ext = extend(factor, fac_halo)

    halo_flux = [dict() for _ in PAIR_OFFSETS]
    for name in fac_halo:
        entry, codes = fac_halo[name], sec_halo[name]
        if isinstance(entry, dict):
            for d in range(len(PAIR_OFFSETS)):
                halo_flux[d][name] = {}
            for m in entry:
                for d, f in enumerate(fibres(codes[m])):
                    halo_flux[d][name][m] = entry[m] * f
        else:
            for d, f in enumerate(fibres(codes)):
                halo_flux[d][name] = entry * f

    beside = {}
    for dy, dz in VARIANTS:
        beside[dy, dz] = [
            None if x is None else jnp.where(x > 0.0, 1.0, 0.0)
            for x in (variant(fac_ext, dy, dz, p) for p in range(lx + 2))
        ]
    for o, (d, offset) in enumerate(OFFSETS):
        dx, dy, dz = offset
        ext = extend(flux[d], halo_flux[d])
        for p in range(lx):
            near = beside[dy, dz][p + 1 + dx]
            c = 0.5 * (flux[d][p] * near + variant(ext, dy, dz, p + 1 + dx) * tissue[p])
            coef[o, p] = c
            diag[p] = c if o == 0 else diag[p] + c
            grad[o, p] = (-0.5 * tissue[p]) * near * fibre[d][p]

    volts_at, gate_at = [], []
    for step in range(WINDOW_STEPS):
        volts_at.append(volts)
        gate_at.append(gate)
        if step:
            stage_fields(step, (volts,))
            send(step)
            drive_v, drive_h = ionic(volts, gate)
        base = volts + tissue * (step_size * drive_v)
        gate = gate + tissue * (step_size * drive_h)
        if step:
            receive(step)
        store_variants(vvar, step, extend(volts, halo(step, 0 if step else 2)))
        volts = jnp.stack(
            [base[p] + tissue[p] * spread(vvar, step, volts[p], p) for p in range(lx)]
        )

    back_v = av_ref[...] + tissue * (volts - rec_ref[...])
    back_h = ah_ref[...]
    terms = jnp.zeros(shape, jnp.float32)

    def add_terms(terms, step, masked):
        rows = []
        for p in range(lx):
            total = terms[p]
            mid_m, mid_v = masked[p], volts_at[step][p]
            for o, (_, offset) in enumerate(OFFSETS):
                total = total + grad[o, p] * (
                    (neighbour(mvar, step, offset, p) - mid_m)
                    * (neighbour(vvar, step, offset, p) - mid_v)
                )
            rows.append(total)
        return jnp.stack(rows)

    pending = None
    phase = WINDOW_STEPS
    for step in reversed(range(WINDOW_STEPS)):
        masked = tissue * back_v
        stage_fields(phase, (masked,))
        send(phase)
        if pending is not None:
            terms = add_terms(terms, *pending)
        vv, vh, hv, hh = partials(volts_at[step], gate_at[step])
        base = back_v + step_size * tissue * (vv * back_v + hv * back_h)
        back_h = back_h + step_size * tissue * (vh * back_v + hh * back_h)
        receive(phase)
        store_variants(mvar, step, extend(masked, halo(phase, 0)))
        if step:
            back_v = jnp.stack(
                [base[p] + spread(mvar, step, masked[p], p) for p in range(lx)]
            )
        pending = (step, masked)
        phase += 1

    terms = add_terms(terms, *pending)
    row = lax.broadcasted_iota(jnp.int32, (8, lz), 0)
    column = lax.broadcasted_iota(jnp.int32, (1, lz), 1)
    sums = jnp.zeros((1, lz), jnp.float32)
    region = region_ref[...]
    for label in range(regions):
        own = jnp.sum(jnp.where(region == label, terms, 0.0), axis=(0, 1))[None]
        own = jnp.sum(own, axis=1, keepdims=True)
        sums = jnp.where(column == label, own, sums)
    gathered[me] = jnp.where(row == 0, jnp.broadcast_to(sums, (8, lz)), 0.0)

    def red_copy(slot, rel):
        return pltpu.make_async_remote_copy(
            src_ref=gathered.at[me],
            dst_ref=gathered.at[slot],
            send_sem=red_send.at[rel],
            recv_sem=red_recv.at[slot],
            device_id=device((me + rel) % n),
            device_id_type=MESH,
        )

    def red_start(rel, carry):
        red_copy(me, rel).start()
        return carry

    def red_wait(rel, carry):
        red_copy((me + rel) % n, rel).wait_recv()
        return carry

    def red_finish(rel, carry):
        red_copy(me, rel).wait_send()
        return carry

    each_other(red_start)
    for p in range(lx):
        out_v[p] = base[p] + spread(mvar, 0, masked[p], p)
    out_h[...] = back_h
    for k in range(len(phase_fields)):
        finish_sends(k)
    each_other(red_wait)
    total = jnp.sum(gathered[...], axis=0)[0:1] * scale
    out_s[...] = total[0, :regions]
    each_other(red_finish)


def local(*args):
    potential, fibre_table, conductance = args[0], args[8], args[9]
    counts = tuple(lax.axis_size(a) for a in ("gx", "gy", "gz"))
    nx, ny, nz = counts
    shape = potential.shape
    lx, ly, lz = shape
    regions, sectors = conductance.shape[0], fibre_table.shape[0]
    cells = lx * ly * lz * nx * ny * nz
    scale = gradient_gain / math.sqrt(cells / regions)
    phase_fields = (3,) + (1,) * (2 * WINDOW_STEPS - 1)
    f32 = jnp.float32
    pairs = len(OFFSETS)
    variants = len(VARIANTS)
    n = nx * ny * nz
    scratch = [
        pltpu.VMEM((pairs,) + shape, f32),
        pltpu.VMEM((pairs,) + shape, f32),
        pltpu.VMEM(shape, f32),
        pltpu.VMEM((WINDOW_STEPS, variants, lx + 2, ly, lz), f32),
        pltpu.VMEM((WINDOW_STEPS, variants, lx + 2, ly, lz), f32),
        pltpu.VMEM((8, lz), f32),
        pltpu.VMEM((n, 8, lz), f32),
        pltpu.SemaphoreType.DMA((n,)),
        pltpu.SemaphoreType.DMA((n,)),
    ]
    moved = messages(ny, nz)
    for fields in phase_fields:
        scratch += [
            pltpu.VMEM((fields, 2, ly, lz), f32),
            pltpu.VMEM((fields, lx, 8, lz), f32),
            pltpu.VMEM((fields, ly, lz), f32),
            pltpu.VMEM((fields, 8, lz), f32),
        ]
        scratch += [pltpu.VMEM(land_shape(move, fields, shape), f32) for move in moved]
        scratch += [pltpu.SemaphoreType.DMA((len(moved),))] * 2
    vmem = pl.BlockSpec(memory_space=pltpu.VMEM)
    smem = pl.BlockSpec(memory_space=pltpu.SMEM)
    return pl.pallas_call(
        functools.partial(kernel, counts, phase_fields, regions, sectors, scale),
        out_shape=(
            jax.ShapeDtypeStruct(shape, f32),
            jax.ShapeDtypeStruct(shape, f32),
            jax.ShapeDtypeStruct((regions,), f32),
        ),
        in_specs=[smem, smem] + [vmem] * 8,
        out_specs=(vmem, vmem, vmem),
        scratch_shapes=scratch,
        compiler_params=pltpu.CompilerParams(
            collective_id=0, has_side_effects=True, vmem_limit_bytes=40 * 2**20
        ),
        name="adjoint_window",
    )(fibre_table, conductance, *args[:8])


def solution(mesh):
    block = P(("twin", "gx"), "gy", "gz")
    in_specs = (block,) * 8 + (P("twin", None), P("twin"))
    out_specs = (block, block, P("twin"))
    return jax.shard_map(local, mesh=mesh, in_specs=in_specs, out_specs=out_specs, check_vma=False)
```

```python
import functools
import math

import jax
import jax.numpy as jnp
from jax import lax
from jax.experimental import pallas as pl
from jax.experimental.pallas import tpu as pltpu
from jax.sharding import PartitionSpec as P

WINDOW_STEPS = 3

step_size = 0.1
tau_inward = 0.3
tau_outward = 6.0
tau_opening = 12.0
tau_closing = 15.0
gate_level = 0.13
gate_width = 0.02
gradient_gain = 30.0
PAIR_OFFSETS = (
    (1, 0, 0),
    (0, 1, 0),
    (0, 0, 1),
    (1, 1, 0),
    (1, -1, 0),
    (1, 0, 1),
    (1, 0, -1),
    (0, 1, 1),
    (0, 1, -1),
)
OFFSETS = tuple(
    (d, tuple(sign * part for part in base))
    for d, base in enumerate(PAIR_OFFSETS)
    for sign in (1, -1)
)
VARIANTS = tuple((dy, dz) for dy in (0, 1, -1) for dz in (0, 1, -1))
FLIP = 2
MESH = pl.DeviceIdType.MESH


def moves(size):
    if size == 1:
        return ()
    return (FLIP,) if size == 2 else (1, -1)


def messages(ny, nz):
    found = []
    for mx in (0, 1, -1):
        for my in (0,) + moves(ny):
            for mz in (0,) + moves(nz):
                if 1 <= (mx != 0) + (my != 0) + (mz != 0) <= 2:
                    found.append((mx, my, mz))
    return sorted(found, key=lambda m: (m[0] == 0, m[2] == 0, m[1] == 0))


def land_shape(move, fields, shape):
    lx, ly, lz = shape
    mx, my, mz = move
    if mz:
        return (fields, 8 if my else ly, lz)
    return (fields, 1 if mx else lx, 8 if my else ly, lz)


def kernel(
    counts,
    phase_fields,
    regions,
    sectors,
    scale,
    *refs,
):
    inputs, refs = refs[:10], refs[10:]
    out_v, out_h, out_s = refs[:3]
    held, (load_sem, *refs) = refs[3:13], refs[13:]
    loads = [
        pltpu.make_async_copy(src, dst, load_sem.at[k])
        for k, (src, dst) in enumerate(zip(inputs, held))
    ]
    for load in loads:
        load.start()
    (region_ref, tissue_ref, cond_ref, sector_ref, v_ref, table_ref, h_ref, av_ref, ah_ref, rec_ref) = held
    (coef, grad, diag, vvar, mvar, gathered, red_send, red_recv, *rest) = refs
    nx, ny, nz = counts
    shape = v_ref.shape
    lx, ly, lz = shape
    moved = messages(ny, nz)
    phases = []
    for _ in phase_fields:
        stage = [rest.pop(0) for _ in range(4)]
        land = {move: rest.pop(0) for move in moved}
        phases.append((stage, land, rest.pop(0), rest.pop(0)))

    ix, iy, iz = lax.axis_index("gx"), lax.axis_index("gy"), lax.axis_index("gz")
    n = nx * ny * nz
    me = (ix * ny + iy) * nz + iz

    def device(index):
        return {"gx": index // (ny * nz), "gy": (index // nz) % ny, "gz": index % nz}

    barrier = pltpu.get_barrier_semaphore()

    def greet(rel, carry):
        pl.semaphore_signal(
            barrier, inc=1, device_id=device((me + rel) % n), device_id_type=MESH
        )
        return carry

    def each_other(body):
        if n <= 64:
            for rel in range(1, n):
                body(rel, 0)
        else:
            lax.fori_loop(1, n, body, 0)

    each_other(greet)

    def along(index, count, move):
        if move == 0:
            return index, None
        if move == FLIP:
            return 1 - index, None
        return index + move, (index < count - 1) if move == 1 else (index > 0)

    def both(conds):
        conds = [c for c in conds if c is not None]
        if not conds:
            return None
        out = conds[0]
        for c in conds[1:]:
            out = jnp.logical_and(out, c)
        return out

    def guarded(cond, body):
        if cond is None:
            body()
        else:
            pl.when(cond)(body)

    def copy_of(phase, k):
        (sx, sy, sz, syz), land, send, recv = phases[phase]
        mx, my, mz = move = moved[k]
        tx, cx = along(ix, nx, mx)
        ty, cy = along(iy, ny, my)
        tz, cz = along(iz, nz, mz)
        back = [along(i, c, m if m == FLIP else -m)[1] for i, c, m in
                ((ix, nx, mx), (iy, ny, my), (iz, nz, mz))]
        if mz:
            src = syz if my else sz
        elif my:
            src = sy
            if mx:
                src = sy.at[:, pl.ds(lx - 1 if mx == 1 else 0, 1)]
        else:
            src = sx.at[:, pl.ds(1 if mx == 1 else 0, 1)]
        copy = pltpu.make_async_remote_copy(
            src_ref=src,
            dst_ref=land[move],
            send_sem=send.at[k],
            recv_sem=recv.at[k],
            device_id={"gx": tx, "gy": ty, "gz": tz},
            device_id_type=MESH,
        )
        return copy, both((cx, cy, cz)), both(back)

    lane3 = lax.broadcasted_iota(jnp.int32, (1, 1, lz), 2)
    sub8 = lax.broadcasted_iota(jnp.int32, (8, lz), 0)
    lane = lax.broadcasted_iota(jnp.int32, (ly, lz), 1)
    lane8 = lax.broadcasted_iota(jnp.int32, (8, lz), 1)

    def roll(x, shift, axis):
        size = x.shape[axis]
        shift = shift % size
        return x if shift == 0 else pltpu.roll(x, shift, axis)

    def stage_fields(phase, fields):
        sx, sy, sz, syz = phases[phase][0]
        for f, u in enumerate(fields):
            sx[f, 0] = u[0]
            sx[f, 1] = u[lx - 1]
            sy[f] = jnp.where((sub8 < 4)[None], u[:, :8], u[:, ly - 8 :])
            packed = jnp.zeros((ly, lz), jnp.float32)
            for p in range(lx):
                edge = jnp.where(lane == 0, roll(u[p], 1, 1), roll(u[p], -1, 1))
                here = (lane == 2 * p) | (lane == 2 * p + 1)
                packed = jnp.where(here, roll(edge, 2 * p + 1, 1), packed)
            sz[f] = packed
            syz[f] = jnp.where(sub8 < 4, packed[:8], packed[ly - 8 :])

    def send(phase):
        for k in range(len(moved)):
            copy, cond, _ = copy_of(phase, k)
            guarded(cond, copy.start)

    def receive(phase):
        for k in range(len(moved)):
            copy, _, cond = copy_of(phase, k)
            guarded(cond, copy.wait_recv)

    def finish_sends(phase):
        for k in range(len(moved)):
            copy, cond, _ = copy_of(phase, k)
            guarded(cond, copy.wait_send)

    one = lambda cond: jnp.where(cond, 1, 0)
    has_x = {1: one(ix > 0), -1: one(ix < nx - 1)}
    yp, ym, zp, zm = one(iy < ny - 1), one(iy > 0), one(iz < nz - 1), one(iz > 0)

    def fetch(phase, f, mx, in_y, in_z):
        land = phases[phase][1]
        rows, lanes = (sub8, lane8) if in_y else (None, lane)
        if in_y:
            y_parts = [
                (m, jnp.where(sub8 < 4, yp if m != 1 else 0, ym if m != -1 else 0))
                for m in moves(ny)
            ]
        else:
            y_parts = [(0, None)]
        if in_z:
            z_parts = [
                (m, jnp.where(lanes % 2 == 0, zp if m != 1 else 0, zm if m != -1 else 0))
                for m in moves(nz)
            ]
        else:
            z_parts = [(0, None)]
        out = None
        for my, cy in y_parts:
            for mz, cz in z_parts:
                value = land[(mx, my, mz)][f]
                ok = has_x[mx] if mx else 1
                for c in (cy, cz):
                    if c is not None:
                        ok = c * ok
                keep = jnp.broadcast_to(ok, value.shape[-2:]) > 0
                if value.ndim == 3:
                    keep = keep[None]
                other = jnp.zeros_like(value) if out is None else out
                out = jnp.where(jnp.broadcast_to(keep, value.shape), value, other)
        return out

    def halo(phase, f):
        return dict(
            x={m: fetch(phase, f, m, False, False)[0] for m in (1, -1)},
            y=fetch(phase, f, 0, True, False),
            xy={m: fetch(phase, f, m, True, False)[0] for m in (1, -1)},
            z=fetch(phase, f, 0, False, True),
            xz={m: fetch(phase, f, m, False, True) for m in (1, -1)},
            yz=fetch(phase, f, 0, True, True),
        )

    def extend(u, parts):
        middle = jnp.concatenate([u, parts["y"]], axis=1)
        ends = {m: jnp.concatenate([parts["x"][m], parts["xy"][m]], axis=0) for m in (1, -1)}
        planes = [ends[1]] + [middle[p] for p in range(lx)] + [ends[-1]]
        z_rows = jnp.concatenate([parts["z"], parts["yz"]], axis=0)
        edges = (
            [roll(parts["xz"][1], -(2 * lx - 1), 1)]
            + [roll(z_rows, -(2 * p + 1), 1) for p in range(lx)]
            + [roll(parts["xz"][-1], -1, 1)]
        )
        return planes, edges

    def variant(ext, dy, dz, p):
        planes, edges = ext
        x = planes[p]
        outer = p in (0, lx + 1)
        if outer and dy and dz:
            return None
        if dz:
            rows = ly if dy == 0 else ly + 8
            at = lax.broadcasted_iota(jnp.int32, (rows, lz), 1)
            x = jnp.where(
                at == (lz - 1 if dz == 1 else 0), edges[p][:rows], roll(x[:rows], -dz, 1)
            )
        if dy:
            x = roll(x, -dy, 0)
        return x[:ly]

    def store_variants(ref, where, ext):
        for k, (dy, dz) in enumerate(VARIANTS):
            for p in range(lx + 2):
                x = variant(ext, dy, dz, p)
                if x is not None:
                    ref[where, k, p] = x

    def neighbour(ref, where, offset, p):
        return ref[where, VARIANTS.index(offset[1:]), p + 1 + offset[0]]

    for load in loads[:5]:
        load.wait()
    tissue = tissue_ref[...].astype(jnp.float32)
    factor = jnp.zeros(shape, jnp.float32)
    for label in range(regions):
        factor = jnp.where(region_ref[...] == label, cond_ref[label], factor)
    factor = tissue * factor
    sector = sector_ref[...].astype(jnp.float32)
    stage_fields(0, (factor, sector, v_ref[...]))
    pl.semaphore_wait(barrier, n - 1)
    send(0)
    for load in loads[5:]:
        load.wait()

    def fibres(codes):
        found = [jnp.zeros(codes.shape, jnp.float32) for _ in PAIR_OFFSETS]
        for label in range(sectors):
            same = codes == float(label)
            for d in range(len(PAIR_OFFSETS)):
                found[d] = jnp.where(same, table_ref[label, d], found[d])
        return found

    def ionic(volts, gate):
        s = 1.0 / (1.0 + jnp.exp(-(volts - gate_level) / gate_width))
        drive_v = gate * volts * volts * (1.0 - volts) / tau_inward - volts / tau_outward
        drive_h = (1.0 - s) * (1.0 - gate) / tau_opening - s * gate / tau_closing
        return drive_v, drive_h

    def partials(volts, gate):
        s = 1.0 / (1.0 + jnp.exp(-(volts - gate_level) / gate_width))
        slope = s * (1.0 - s) / gate_width
        vv = gate * (2.0 * volts - 3.0 * volts * volts) / tau_inward - 1.0 / tau_outward
        vh = volts * volts * (1.0 - volts) / tau_inward
        hv = slope * (-(1.0 - gate) / tau_opening - gate / tau_closing)
        hh = -(1.0 - s) / tau_opening - s / tau_closing
        return vv, vh, hv, hh

    def spread(ref, where, u, p):
        total = -diag[p] * u
        for o, (_, offset) in enumerate(OFFSETS):
            total = total + coef[o, p] * neighbour(ref, where, offset, p)
        return total

    fibre = fibres(sector)
    flux = [factor * f for f in fibre]
    volts, gate = v_ref[...], h_ref[...]
    drive_v, drive_h = ionic(volts, gate)

    receive(0)
    fac_halo = halo(0, 0)
    sec_halo = halo(0, 1)
    fac_ext = extend(factor, fac_halo)

    halo_flux = [dict() for _ in PAIR_OFFSETS]
    for name in fac_halo:
        entry, codes = fac_halo[name], sec_halo[name]
        if isinstance(entry, dict):
            for d in range(len(PAIR_OFFSETS)):
                halo_flux[d][name] = {}
            for m in entry:
                for d, f in enumerate(fibres(codes[m])):
                    halo_flux[d][name][m] = entry[m] * f
        else:
            for d, f in enumerate(fibres(codes)):
                halo_flux[d][name] = entry * f

    beside = {}
    for dy, dz in VARIANTS:
        beside[dy, dz] = [
            None if x is None else jnp.where(x > 0.0, 1.0, 0.0)
            for x in (variant(fac_ext, dy, dz, p) for p in range(lx + 2))
        ]
    for o, (d, offset) in enumerate(OFFSETS):
        dx, dy, dz = offset
        ext = extend(flux[d], halo_flux[d])
        for p in range(lx):
            near = beside[dy, dz][p + 1 + dx]
            c = 0.5 * (flux[d][p] * near + variant(ext, dy, dz, p + 1 + dx) * tissue[p])
            coef[o, p] = c
            diag[p] = c if o == 0 else diag[p] + c
            grad[o, p] = (-0.5 * tissue[p]) * near * fibre[d][p]

    volts_at, gate_at = [], []
    for step in range(WINDOW_STEPS):
        volts_at.append(volts)
        gate_at.append(gate)
        if step:
            stage_fields(step, (volts,))
            send(step)
            drive_v, drive_h = ionic(volts, gate)
        base = volts + tissue * (step_size * drive_v)
        gate = gate + tissue * (step_size * drive_h)
        if step:
            receive(step)
        store_variants(vvar, step, extend(volts, halo(step, 0 if step else 2)))
        volts = jnp.stack(
            [base[p] + tissue[p] * spread(vvar, step, volts[p], p) for p in range(lx)]
        )

    back_v = av_ref[...] + tissue * (volts - rec_ref[...])
    back_h = ah_ref[...]
    terms = jnp.zeros(shape, jnp.float32)

    def add_terms(terms, step, masked):
        rows = []
        for p in range(lx):
            total = terms[p]
            mid_m, mid_v = masked[p], volts_at[step][p]
            for o, (_, offset) in enumerate(OFFSETS):
                total = total + grad[o, p] * (
                    (neighbour(mvar, step, offset, p) - mid_m)
                    * (neighbour(vvar, step, offset, p) - mid_v)
                )
            rows.append(total)
        return jnp.stack(rows)

    pending = None
    phase = WINDOW_STEPS
    for step in reversed(range(WINDOW_STEPS)):
        masked = tissue * back_v
        stage_fields(phase, (masked,))
        send(phase)
        if pending is not None:
            terms = add_terms(terms, *pending)
        vv, vh, hv, hh = partials(volts_at[step], gate_at[step])
        base = back_v + step_size * tissue * (vv * back_v + hv * back_h)
        back_h = back_h + step_size * tissue * (vh * back_v + hh * back_h)
        receive(phase)
        store_variants(mvar, step, extend(masked, halo(phase, 0)))
        if step:
            back_v = jnp.stack(
                [base[p] + spread(mvar, step, masked[p], p) for p in range(lx)]
            )
        pending = (step, masked)
        phase += 1

    terms = add_terms(terms, *pending)
    row = lax.broadcasted_iota(jnp.int32, (8, lz), 0)
    column = lax.broadcasted_iota(jnp.int32, (1, lz), 1)
    sums = jnp.zeros((1, lz), jnp.float32)
    region = region_ref[...]
    for label in range(regions):
        own = jnp.sum(jnp.where(region == label, terms, 0.0), axis=(0, 1))[None]
        own = jnp.sum(own, axis=1, keepdims=True)
        sums = jnp.where(column == label, own, sums)
    gathered[me] = jnp.where(row == 0, jnp.broadcast_to(sums, (8, lz)), 0.0)

    def red_copy(slot, rel):
        return pltpu.make_async_remote_copy(
            src_ref=gathered.at[me],
            dst_ref=gathered.at[slot],
            send_sem=red_send.at[rel],
            recv_sem=red_recv.at[slot],
            device_id=device((me + rel) % n),
            device_id_type=MESH,
        )

    def red_start(rel, carry):
        red_copy(me, rel).start()
        return carry

    def red_wait(rel, carry):
        red_copy((me + rel) % n, rel).wait_recv()
        return carry

    def red_finish(rel, carry):
        red_copy(me, rel).wait_send()
        return carry

    each_other(red_start)
    for p in range(lx):
        out_v[p] = base[p] + spread(mvar, 0, masked[p], p)
    out_h[...] = back_h
    for k in range(len(phase_fields)):
        finish_sends(k)
    each_other(red_wait)
    total = jnp.sum(gathered[...], axis=0)[0:1] * scale
    out_s[...] = total[0, :regions]
    each_other(red_finish)


def local(*args):
    potential, fibre_table, conductance = args[0], args[8], args[9]
    counts = tuple(lax.axis_size(a) for a in ("gx", "gy", "gz"))
    nx, ny, nz = counts
    shape = potential.shape
    lx, ly, lz = shape
    regions, sectors = conductance.shape[0], fibre_table.shape[0]
    cells = lx * ly * lz * nx * ny * nz
    scale = gradient_gain / math.sqrt(cells / regions)
    phase_fields = (3,) + (1,) * (2 * WINDOW_STEPS - 1)
    f32 = jnp.float32
    pairs = len(OFFSETS)
    variants = len(VARIANTS)
    n = nx * ny * nz
    order = (7, 5, 9, 6, 0, 8, 1, 2, 3, 4)
    operands = [args[k] for k in order]
    scratch = [
        (pltpu.SMEM if k >= 8 else pltpu.VMEM)(args[k].shape, args[k].dtype) for k in order
    ]
    scratch += [
        pltpu.SemaphoreType.DMA((len(order),)),
        pltpu.VMEM((pairs,) + shape, f32),
        pltpu.VMEM((pairs,) + shape, f32),
        pltpu.VMEM(shape, f32),
        pltpu.VMEM((WINDOW_STEPS, variants, lx + 2, ly, lz), f32),
        pltpu.VMEM((WINDOW_STEPS, variants, lx + 2, ly, lz), f32),
        pltpu.VMEM((n, 8, lz), f32),
        pltpu.SemaphoreType.DMA((n,)),
        pltpu.SemaphoreType.DMA((n,)),
    ]
    moved = messages(ny, nz)
    for fields in phase_fields:
        scratch += [
            pltpu.VMEM((fields, 2, ly, lz), f32),
            pltpu.VMEM((fields, lx, 8, lz), f32),
            pltpu.VMEM((fields, ly, lz), f32),
            pltpu.VMEM((fields, 8, lz), f32),
        ]
        scratch += [pltpu.VMEM(land_shape(move, fields, shape), f32) for move in moved]
        scratch += [pltpu.SemaphoreType.DMA((len(moved),))] * 2
    vmem = pl.BlockSpec(memory_space=pltpu.VMEM)
    hbm = pl.BlockSpec(memory_space=pltpu.HBM)
    return pl.pallas_call(
        functools.partial(kernel, counts, phase_fields, regions, sectors, scale),
        out_shape=(
            jax.ShapeDtypeStruct(shape, f32),
            jax.ShapeDtypeStruct(shape, f32),
            jax.ShapeDtypeStruct((regions,), f32),
        ),
        in_specs=[hbm] * len(order),
        out_specs=(vmem, vmem, vmem),
        scratch_shapes=scratch,
        compiler_params=pltpu.CompilerParams(
            collective_id=0, has_side_effects=True, vmem_limit_bytes=40 * 2**20
        ),
        name="adjoint_window",
    )(*operands)


def solution(mesh):
    block = P(("twin", "gx"), "gy", "gz")
    in_specs = (block,) * 8 + (P("twin", None), P("twin"))
    out_specs = (block, block, P("twin"))
    return jax.shard_map(local, mesh=mesh, in_specs=in_specs, out_specs=out_specs, check_vma=False)
```

```python
import functools
import math

import jax
import jax.numpy as jnp
from jax import lax
from jax.experimental import pallas as pl
from jax.experimental.pallas import tpu as pltpu
from jax.sharding import PartitionSpec as P

WINDOW_STEPS = 3

step_size = 0.1
tau_inward = 0.3
tau_outward = 6.0
tau_opening = 12.0
tau_closing = 15.0
gate_level = 0.13
gate_width = 0.02
gradient_gain = 30.0
PAIR_OFFSETS = (
    (1, 0, 0),
    (0, 1, 0),
    (0, 0, 1),
    (1, 1, 0),
    (1, -1, 0),
    (1, 0, 1),
    (1, 0, -1),
    (0, 1, 1),
    (0, 1, -1),
)
OFFSETS = tuple(
    (d, tuple(sign * part for part in base))
    for d, base in enumerate(PAIR_OFFSETS)
    for sign in (1, -1)
)
VARIANTS = tuple((dy, dz) for dy in (0, 1, -1) for dz in (0, 1, -1))
FLIP = 2
MESH = pl.DeviceIdType.MESH


def moves(size):
    if size == 1:
        return ()
    return (FLIP,) if size == 2 else (1, -1)


def messages(ny, nz):
    found = []
    for mx in (0, 1, -1):
        for my in (0,) + moves(ny):
            for mz in (0,) + moves(nz):
                if 1 <= (mx != 0) + (my != 0) + (mz != 0) <= 2:
                    found.append((mx, my, mz))
    return sorted(found, key=lambda m: (m[0] == 0, m[2] == 0, m[1] == 0))


def land_shape(move, fields, shape):
    lx, ly, lz = shape
    mx, my, mz = move
    if mz:
        return (fields, 8 if my else ly, lz)
    return (fields, 1 if mx else lx, 8 if my else ly, lz)


def kernel(
    counts,
    phase_fields,
    regions,
    sectors,
    scale,
    *refs,
):
    inputs, refs = refs[:10], refs[10:]
    out_v, out_h, out_s = refs[:3]
    held, (load_sem, *refs) = refs[3:13], refs[13:]
    loads = [
        pltpu.make_async_copy(src, dst, load_sem.at[k])
        for k, (src, dst) in enumerate(zip(inputs, held))
    ]
    for load in loads:
        load.start()
    (region_ref, tissue_ref, cond_ref, sector_ref, v_ref, table_ref, h_ref, av_ref, ah_ref, rec_ref) = held
    (coef, grad, diag, vvar, mvar, gathered, red_send, red_recv, *rest) = refs
    nx, ny, nz = counts
    shape = v_ref.shape
    lx, ly, lz = shape
    moved = messages(ny, nz)
    phases = []
    for _ in phase_fields:
        stage = [rest.pop(0) for _ in range(4)]
        land = {move: rest.pop(0) for move in moved}
        phases.append((stage, land, rest.pop(0), rest.pop(0)))

    ix, iy, iz = lax.axis_index("gx"), lax.axis_index("gy"), lax.axis_index("gz")
    n = nx * ny * nz
    me = (ix * ny + iy) * nz + iz

    def device(index):
        return {"gx": index // (ny * nz), "gy": (index // nz) % ny, "gz": index % nz}

    barrier = pltpu.get_barrier_semaphore()

    def greet(rel, carry):
        pl.semaphore_signal(
            barrier, inc=1, device_id=device((me + rel) % n), device_id_type=MESH
        )
        return carry

    def each_other(body):
        if n <= 64:
            for rel in range(1, n):
                body(rel, 0)
        else:
            lax.fori_loop(1, n, body, 0)

    each_other(greet)

    def along(index, count, move):
        if move == 0:
            return index, None
        if move == FLIP:
            return 1 - index, None
        return index + move, (index < count - 1) if move == 1 else (index > 0)

    def both(conds):
        conds = [c for c in conds if c is not None]
        if not conds:
            return None
        out = conds[0]
        for c in conds[1:]:
            out = jnp.logical_and(out, c)
        return out

    def guarded(cond, body):
        if cond is None:
            body()
        else:
            pl.when(cond)(body)

    def copy_of(phase, k):
        (sx, sy, sz, syz), land, send, recv = phases[phase]
        mx, my, mz = move = moved[k]
        tx, cx = along(ix, nx, mx)
        ty, cy = along(iy, ny, my)
        tz, cz = along(iz, nz, mz)
        back = [along(i, c, m if m == FLIP else -m)[1] for i, c, m in
                ((ix, nx, mx), (iy, ny, my), (iz, nz, mz))]
        if mz:
            src = syz if my else sz
        elif my:
            src = sy
            if mx:
                src = sy.at[:, pl.ds(lx - 1 if mx == 1 else 0, 1)]
        else:
            src = sx.at[:, pl.ds(1 if mx == 1 else 0, 1)]
        copy = pltpu.make_async_remote_copy(
            src_ref=src,
            dst_ref=land[move],
            send_sem=send.at[k],
            recv_sem=recv.at[k],
            device_id={"gx": tx, "gy": ty, "gz": tz},
            device_id_type=MESH,
        )
        return copy, both((cx, cy, cz)), both(back)

    lane3 = lax.broadcasted_iota(jnp.int32, (1, 1, lz), 2)
    sub8 = lax.broadcasted_iota(jnp.int32, (8, lz), 0)
    lane = lax.broadcasted_iota(jnp.int32, (ly, lz), 1)
    lane8 = lax.broadcasted_iota(jnp.int32, (8, lz), 1)

    def roll(x, shift, axis):
        size = x.shape[axis]
        shift = shift % size
        return x if shift == 0 else pltpu.roll(x, shift, axis)

    def stage_fields(phase, fields):
        sx, sy, sz, syz = phases[phase][0]
        for f, u in enumerate(fields):
            sx[f, 0] = u[0]
            sx[f, 1] = u[lx - 1]
            sy[f] = jnp.where((sub8 < 4)[None], u[:, :8], u[:, ly - 8 :])
            packed = jnp.zeros((ly, lz), jnp.float32)
            for p in range(lx):
                edge = jnp.where(lane == 0, roll(u[p], 1, 1), roll(u[p], -1, 1))
                here = (lane == 2 * p) | (lane == 2 * p + 1)
                packed = jnp.where(here, roll(edge, 2 * p + 1, 1), packed)
            sz[f] = packed
            syz[f] = jnp.where(sub8 < 4, packed[:8], packed[ly - 8 :])

    def send(phase):
        for k in range(len(moved)):
            copy, cond, _ = copy_of(phase, k)
            guarded(cond, copy.start)

    def receive(phase):
        for k in range(len(moved)):
            copy, _, cond = copy_of(phase, k)
            guarded(cond, copy.wait_recv)

    def finish_sends(phase):
        for k in range(len(moved)):
            copy, cond, _ = copy_of(phase, k)
            guarded(cond, copy.wait_send)

    one = lambda cond: jnp.where(cond, 1, 0)
    has_x = {1: one(ix > 0), -1: one(ix < nx - 1)}
    yp, ym, zp, zm = one(iy < ny - 1), one(iy > 0), one(iz < nz - 1), one(iz > 0)

    def fetch(phase, f, mx, in_y, in_z):
        land = phases[phase][1]
        rows, lanes = (sub8, lane8) if in_y else (None, lane)
        if in_y:
            y_parts = [
                (m, jnp.where(sub8 < 4, yp if m != 1 else 0, ym if m != -1 else 0))
                for m in moves(ny)
            ]
        else:
            y_parts = [(0, None)]
        if in_z:
            z_parts = [
                (m, jnp.where(lanes % 2 == 0, zp if m != 1 else 0, zm if m != -1 else 0))
                for m in moves(nz)
            ]
        else:
            z_parts = [(0, None)]
        out = None
        for my, cy in y_parts:
            for mz, cz in z_parts:
                value = land[(mx, my, mz)][f]
                ok = has_x[mx] if mx else 1
                for c in (cy, cz):
                    if c is not None:
                        ok = c * ok
                keep = jnp.broadcast_to(ok, value.shape[-2:]) > 0
                if value.ndim == 3:
                    keep = keep[None]
                other = jnp.zeros_like(value) if out is None else out
                out = jnp.where(jnp.broadcast_to(keep, value.shape), value, other)
        return out

    def halo(phase, f):
        return dict(
            x={m: fetch(phase, f, m, False, False)[0] for m in (1, -1)},
            y=fetch(phase, f, 0, True, False),
            xy={m: fetch(phase, f, m, True, False)[0] for m in (1, -1)},
            z=fetch(phase, f, 0, False, True),
            xz={m: fetch(phase, f, m, False, True) for m in (1, -1)},
            yz=fetch(phase, f, 0, True, True),
        )

    def extend(u, parts):
        middle = jnp.concatenate([u, parts["y"]], axis=1)
        ends = {m: jnp.concatenate([parts["x"][m], parts["xy"][m]], axis=0) for m in (1, -1)}
        planes = [ends[1]] + [middle[p] for p in range(lx)] + [ends[-1]]
        z_rows = jnp.concatenate([parts["z"], parts["yz"]], axis=0)
        edges = (
            [roll(parts["xz"][1], -(2 * lx - 1), 1)]
            + [roll(z_rows, -(2 * p + 1), 1) for p in range(lx)]
            + [roll(parts["xz"][-1], -1, 1)]
        )
        return planes, edges

    def variant(ext, dy, dz, p):
        planes, edges = ext
        x = planes[p]
        outer = p in (0, lx + 1)
        if outer and dy and dz:
            return None
        if dz:
            rows = ly if dy == 0 else ly + 8
            at = lax.broadcasted_iota(jnp.int32, (rows, lz), 1)
            x = jnp.where(
                at == (lz - 1 if dz == 1 else 0), edges[p][:rows], roll(x[:rows], -dz, 1)
            )
        if dy:
            x = roll(x, -dy, 0)
        return x[:ly]

    def store_variants(ref, where, ext):
        for k, (dy, dz) in enumerate(VARIANTS):
            for p in range(lx + 2):
                x = variant(ext, dy, dz, p)
                if x is not None:
                    ref[where, k, p] = x

    def neighbour(ref, where, offset, p):
        return ref[where, VARIANTS.index(offset[1:]), p + 1 + offset[0]]

    for load in loads[:5]:
        load.wait()
    tissue = tissue_ref[...].astype(jnp.float32)
    factor = jnp.zeros(shape, jnp.float32)
    for label in range(regions):
        factor = jnp.where(region_ref[...] == label, cond_ref[label], factor)
    factor = tissue * factor
    sector = sector_ref[...].astype(jnp.float32)
    stage_fields(0, (factor, sector, v_ref[...]))
    pl.semaphore_wait(barrier, n - 1)
    send(0)
    for load in loads[5:]:
        load.wait()

    def fibres(codes):
        found = [jnp.zeros(codes.shape, jnp.float32) for _ in PAIR_OFFSETS]
        for label in range(sectors):
            same = codes == float(label)
            for d in range(len(PAIR_OFFSETS)):
                found[d] = jnp.where(same, table_ref[label, d], found[d])
        return found

    def ionic(volts, gate):
        s = 1.0 / (1.0 + jnp.exp(-(volts - gate_level) / gate_width))
        drive_v = gate * volts * volts * (1.0 - volts) / tau_inward - volts / tau_outward
        drive_h = (1.0 - s) * (1.0 - gate) / tau_opening - s * gate / tau_closing
        return drive_v, drive_h

    def partials(volts, gate):
        s = 1.0 / (1.0 + jnp.exp(-(volts - gate_level) / gate_width))
        slope = s * (1.0 - s) / gate_width
        vv = gate * (2.0 * volts - 3.0 * volts * volts) / tau_inward - 1.0 / tau_outward
        vh = volts * volts * (1.0 - volts) / tau_inward
        hv = slope * (-(1.0 - gate) / tau_opening - gate / tau_closing)
        hh = -(1.0 - s) / tau_opening - s / tau_closing
        return vv, vh, hv, hh

    def spread(ref, where, u, p):
        total = -diag[p] * u
        for o, (_, offset) in enumerate(OFFSETS):
            total = total + coef[o, p] * neighbour(ref, where, offset, p)
        return total

    fibre = fibres(sector)
    flux = [factor * f for f in fibre]
    volts, gate = v_ref[...], h_ref[...]
    drive_v, drive_h = ionic(volts, gate)

    receive(0)
    fac_halo = halo(0, 0)
    sec_halo = halo(0, 1)
    fac_ext = extend(factor, fac_halo)

    halo_flux = [dict() for _ in PAIR_OFFSETS]
    for name in fac_halo:
        entry, codes = fac_halo[name], sec_halo[name]
        if isinstance(entry, dict):
            for d in range(len(PAIR_OFFSETS)):
                halo_flux[d][name] = {}
            for m in entry:
                for d, f in enumerate(fibres(codes[m])):
                    halo_flux[d][name][m] = entry[m] * f
        else:
            for d, f in enumerate(fibres(codes)):
                halo_flux[d][name] = entry * f

    beside = {}
    for dy, dz in VARIANTS:
        beside[dy, dz] = [
            None if x is None else jnp.where(x > 0.0, 1.0, 0.0)
            for x in (variant(fac_ext, dy, dz, p) for p in range(lx + 2))
        ]
    for o, (d, offset) in enumerate(OFFSETS):
        dx, dy, dz = offset
        ext = extend(flux[d], halo_flux[d])
        for p in range(lx):
            near = beside[dy, dz][p + 1 + dx]
            c = 0.5 * (flux[d][p] * near + variant(ext, dy, dz, p + 1 + dx) * tissue[p])
            coef[o, p] = c
            diag[p] = c if o == 0 else diag[p] + c
            grad[o, p] = (-0.5 * tissue[p]) * near * fibre[d][p]

    volts_at, gate_at = [], []
    for step in range(WINDOW_STEPS):
        volts_at.append(volts)
        gate_at.append(gate)
        if step:
            stage_fields(step, (volts,))
            send(step)
            drive_v, drive_h = ionic(volts, gate)
        base = volts + tissue * (step_size * drive_v)
        gate = gate + tissue * (step_size * drive_h)
        if step:
            receive(step)
        store_variants(vvar, step, extend(volts, halo(step, 0 if step else 2)))
        volts = jnp.stack(
            [base[p] + tissue[p] * spread(vvar, step, volts[p], p) for p in range(lx)]
        )

    back_v = av_ref[...] + tissue * (volts - rec_ref[...])
    back_h = ah_ref[...]
    terms = jnp.zeros(shape, jnp.float32)

    def add_terms(terms, step, masked):
        rows = []
        for p in range(lx):
            total = terms[p]
            mid_m, mid_v = masked[p], volts_at[step][p]
            for o, (_, offset) in enumerate(OFFSETS):
                total = total + grad[o, p] * (
                    (neighbour(mvar, step, offset, p) - mid_m)
                    * (neighbour(vvar, step, offset, p) - mid_v)
                )
            rows.append(total)
        return jnp.stack(rows)

    pending = None
    phase = WINDOW_STEPS
    for step in reversed(range(WINDOW_STEPS)):
        masked = tissue * back_v
        stage_fields(phase, (masked,))
        send(phase)
        if pending is not None:
            terms = add_terms(terms, *pending)
        vv, vh, hv, hh = partials(volts_at[step], gate_at[step])
        base = back_v + step_size * tissue * (vv * back_v + hv * back_h)
        back_h = back_h + step_size * tissue * (vh * back_v + hh * back_h)
        receive(phase)
        store_variants(mvar, step, extend(masked, halo(phase, 0)))
        if step:
            back_v = jnp.stack(
                [base[p] + spread(mvar, step, masked[p], p) for p in range(lx)]
            )
        pending = (step, masked)
        phase += 1

    terms = add_terms(terms, *pending)
    row = lax.broadcasted_iota(jnp.int32, (8, lz), 0)
    column = lax.broadcasted_iota(jnp.int32, (1, lz), 1)
    sums = jnp.zeros((1, lz), jnp.float32)
    region = region_ref[...]
    for label in range(regions):
        own = jnp.sum(jnp.where(region == label, terms, 0.0), axis=(0, 1))[None]
        own = jnp.sum(own, axis=1, keepdims=True)
        sums = jnp.where(column == label, own, sums)
    gathered[me] = jnp.where(row == 0, jnp.broadcast_to(sums, (8, lz)), 0.0)

    def red_copy(slot, rel):
        return pltpu.make_async_remote_copy(
            src_ref=gathered.at[me],
            dst_ref=gathered.at[slot],
            send_sem=red_send.at[rel],
            recv_sem=red_recv.at[slot],
            device_id=device((me + rel) % n),
            device_id_type=MESH,
        )

    def red_start(rel, carry):
        red_copy(me, rel).start()
        return carry

    def red_wait(rel, carry):
        red_copy((me + rel) % n, rel).wait_recv()
        return carry

    def red_finish(rel, carry):
        red_copy(me, rel).wait_send()
        return carry

    each_other(red_start)
    for p in range(lx):
        out_v[p] = base[p] + spread(mvar, 0, masked[p], p)
    out_h[...] = back_h
    for k in range(len(phase_fields)):
        finish_sends(k)
    each_other(red_wait)
    total = jnp.sum(gathered[...], axis=0)[0:1] * scale
    out_s[...] = total[0, :regions]
    each_other(red_finish)


def local(*args):
    potential, fibre_table, conductance = args[0], args[8], args[9]
    counts = tuple(lax.axis_size(a) for a in ("gx", "gy", "gz"))
    nx, ny, nz = counts
    shape = potential.shape
    lx, ly, lz = shape
    regions, sectors = conductance.shape[0], fibre_table.shape[0]
    cells = lx * ly * lz * nx * ny * nz
    scale = gradient_gain / math.sqrt(cells / regions)
    phase_fields = (3,) + (1,) * (2 * WINDOW_STEPS - 1)
    f32 = jnp.float32
    pairs = len(OFFSETS)
    variants = len(VARIANTS)
    n = nx * ny * nz
    order = (7, 5, 9, 6, 0, 8, 1, 2, 3, 4)
    operands = [args[k] for k in order]
    scratch = [
        (pltpu.SMEM if k >= 8 else pltpu.VMEM)(args[k].shape, args[k].dtype) for k in order
    ]
    scratch += [
        pltpu.SemaphoreType.DMA((len(order),)),
        pltpu.VMEM((pairs,) + shape, f32),
        pltpu.VMEM((pairs,) + shape, f32),
        pltpu.VMEM(shape, f32),
        pltpu.VMEM((WINDOW_STEPS, variants, lx + 2, ly, lz), f32),
        pltpu.VMEM((WINDOW_STEPS, variants, lx + 2, ly, lz), f32),
        pltpu.VMEM((n, 8, lz), f32),
        pltpu.SemaphoreType.DMA((n,)),
        pltpu.SemaphoreType.DMA((n,)),
    ]
    moved = messages(ny, nz)
    for fields in phase_fields:
        scratch += [
            pltpu.VMEM((fields, 2, ly, lz), f32),
            pltpu.VMEM((fields, lx, 8, lz), f32),
            pltpu.VMEM((fields, ly, lz), f32),
            pltpu.VMEM((fields, 8, lz), f32),
        ]
        scratch += [pltpu.VMEM(land_shape(move, fields, shape), f32) for move in moved]
        scratch += [pltpu.SemaphoreType.DMA((len(moved),))] * 2
    vmem = pl.BlockSpec(memory_space=pltpu.VMEM)
    hbm = pl.BlockSpec(memory_space=pltpu.HBM)
    return pl.pallas_call(
        functools.partial(kernel, counts, phase_fields, regions, sectors, scale),
        out_shape=(
            jax.ShapeDtypeStruct(shape, f32),
            jax.ShapeDtypeStruct(shape, f32),
            jax.ShapeDtypeStruct((regions,), f32),
        ),
        in_specs=[hbm] * len(order),
        out_specs=(vmem, vmem, vmem),
        scratch_shapes=scratch,
        compiler_params=pltpu.CompilerParams(
            collective_id=0, has_side_effects=True, vmem_limit_bytes=63 * 2**20
        ),
        name="adjoint_window",
    )(*operands)


def solution(mesh):
    block = P(("twin", "gx"), "gy", "gz")
    in_specs = (block,) * 8 + (P("twin", None), P("twin"))
    out_specs = (block, block, P("twin"))
    return jax.shard_map(local, mesh=mesh, in_specs=in_specs, out_specs=out_specs, check_vma=False)
```

```python
import functools
import math

import jax
import jax.numpy as jnp
from jax import lax
from jax.experimental import pallas as pl
from jax.experimental.pallas import tpu as pltpu
from jax.sharding import PartitionSpec as P

WINDOW_STEPS = 3

step_size = 0.1
tau_inward = 0.3
tau_outward = 6.0
tau_opening = 12.0
tau_closing = 15.0
gate_level = 0.13
gate_width = 0.02
gradient_gain = 30.0
PAIR_OFFSETS = (
    (1, 0, 0),
    (0, 1, 0),
    (0, 0, 1),
    (1, 1, 0),
    (1, -1, 0),
    (1, 0, 1),
    (1, 0, -1),
    (0, 1, 1),
    (0, 1, -1),
)
OFFSETS = tuple(
    (d, tuple(sign * part for part in base))
    for d, base in enumerate(PAIR_OFFSETS)
    for sign in (1, -1)
)
VARIANTS = tuple((dy, dz) for dy in (0, 1, -1) for dz in (0, 1, -1))
FLIP = 2
MESH = pl.DeviceIdType.MESH


def moves(size):
    if size == 1:
        return ()
    return (FLIP,) if size == 2 else (1, -1)


def messages(ny, nz):
    found = []
    for mx in (0, 1, -1):
        for my in (0,) + moves(ny):
            for mz in (0,) + moves(nz):
                if 1 <= (mx != 0) + (my != 0) + (mz != 0) <= 2:
                    found.append((mx, my, mz))
    return sorted(found, key=lambda m: (m[0] == 0, m[2] == 0, m[1] == 0))


def land_shape(move, fields, shape):
    lx, ly, lz = shape
    mx, my, mz = move
    if mz:
        return (fields, 8 if my else ly, lz)
    return (fields, 1 if mx else lx, 8 if my else ly, lz)


def kernel(
    counts,
    phase_fields,
    regions,
    sectors,
    scale,
    *refs,
):
    inputs, refs = refs[:10], refs[10:]
    out_v, out_h, out_s = refs[:3]
    held, (load_sem, *refs) = refs[3:13], refs[13:]
    loads = [
        pltpu.make_async_copy(src, dst, load_sem.at[k])
        for k, (src, dst) in enumerate(zip(inputs, held))
    ]
    for load in loads:
        load.start()
    (region_ref, tissue_ref, cond_ref, sector_ref, v_ref, table_ref, h_ref, av_ref, ah_ref, rec_ref) = held
    (final_v, final_h, final_s, save_sem, *refs) = refs
    (coef, grad, diag, vvar, mvar, gathered, red_send, red_recv, *rest) = refs
    nx, ny, nz = counts
    shape = v_ref.shape
    lx, ly, lz = shape
    moved = messages(ny, nz)
    phases = []
    for _ in phase_fields:
        stage = [rest.pop(0) for _ in range(4)]
        land = {move: rest.pop(0) for move in moved}
        phases.append((stage, land, rest.pop(0), rest.pop(0)))

    ix, iy, iz = lax.axis_index("gx"), lax.axis_index("gy"), lax.axis_index("gz")
    n = nx * ny * nz
    me = (ix * ny + iy) * nz + iz

    def device(index):
        return {"gx": index // (ny * nz), "gy": (index // nz) % ny, "gz": index % nz}

    barrier = pltpu.get_barrier_semaphore()

    def wrapped(index, count, by):
        if by == 0:
            return index
        moved_on = index + by
        return jnp.where(moved_on >= count, moved_on - count, moved_on)

    def greet(rel, slot, target):
        pl.semaphore_signal(barrier, inc=1, device_id=target, device_id_type=MESH)

    def each_other(body):
        if n <= 64:
            for rel in range(n - 1, 0, -1):
                tx = wrapped(ix, nx, rel // (ny * nz))
                ty = wrapped(iy, ny, rel // nz % ny)
                tz = wrapped(iz, nz, rel % nz)
                body(rel, (tx * ny + ty) * nz + tz, {"gx": tx, "gy": ty, "gz": tz})
        else:

            def step(rel, carry):
                slot = (me + rel) % n
                body(rel, slot, device(slot))
                return carry

            lax.fori_loop(1, n, step, 0)

    each_other(greet)

    def along(index, count, move):
        if move == 0:
            return index, None
        if move == FLIP:
            return 1 - index, None
        return index + move, (index < count - 1) if move == 1 else (index > 0)

    def both(conds):
        conds = [c for c in conds if c is not None]
        if not conds:
            return None
        out = conds[0]
        for c in conds[1:]:
            out = jnp.logical_and(out, c)
        return out

    def guarded(cond, body):
        if cond is None:
            body()
        else:
            pl.when(cond)(body)

    def copy_of(phase, k):
        (sx, sy, sz, syz), land, send, recv = phases[phase]
        mx, my, mz = move = moved[k]
        tx, cx = along(ix, nx, mx)
        ty, cy = along(iy, ny, my)
        tz, cz = along(iz, nz, mz)
        back = [along(i, c, m if m == FLIP else -m)[1] for i, c, m in
                ((ix, nx, mx), (iy, ny, my), (iz, nz, mz))]
        if mz:
            src = syz if my else sz
        elif my:
            src = sy
            if mx:
                src = sy.at[:, pl.ds(lx - 1 if mx == 1 else 0, 1)]
        else:
            src = sx.at[:, pl.ds(1 if mx == 1 else 0, 1)]
        copy = pltpu.make_async_remote_copy(
            src_ref=src,
            dst_ref=land[move],
            send_sem=send.at[k],
            recv_sem=recv.at[k],
            device_id={"gx": tx, "gy": ty, "gz": tz},
            device_id_type=MESH,
        )
        return copy, both((cx, cy, cz)), both(back)

    lane3 = lax.broadcasted_iota(jnp.int32, (1, 1, lz), 2)
    sub8 = lax.broadcasted_iota(jnp.int32, (8, lz), 0)
    lane = lax.broadcasted_iota(jnp.int32, (ly, lz), 1)
    lane8 = lax.broadcasted_iota(jnp.int32, (8, lz), 1)

    def roll(x, shift, axis):
        size = x.shape[axis]
        shift = shift % size
        return x if shift == 0 else pltpu.roll(x, shift, axis)

    def stage_fields(phase, fields):
        sx, sy, sz, syz = phases[phase][0]
        for f, u in enumerate(fields):
            sx[f, 0] = u[0]
            sx[f, 1] = u[lx - 1]
            sy[f] = jnp.where((sub8 < 4)[None], u[:, :8], u[:, ly - 8 :])
            packed = jnp.zeros((ly, lz), jnp.float32)
            for p in range(lx):
                edge = jnp.where(lane == 0, roll(u[p], 1, 1), roll(u[p], -1, 1))
                here = (lane == 2 * p) | (lane == 2 * p + 1)
                packed = jnp.where(here, roll(edge, 2 * p + 1, 1), packed)
            sz[f] = packed
            syz[f] = jnp.where(sub8 < 4, packed[:8], packed[ly - 8 :])

    def send(phase):
        for k in range(len(moved)):
            copy, cond, _ = copy_of(phase, k)
            guarded(cond, copy.start)

    def receive(phase):
        for k in range(len(moved)):
            copy, _, cond = copy_of(phase, k)
            guarded(cond, copy.wait_recv)

    def finish_sends(phase):
        for k in range(len(moved)):
            copy, cond, _ = copy_of(phase, k)
            guarded(cond, copy.wait_send)

    one = lambda cond: jnp.where(cond, 1, 0)
    has_x = {1: one(ix > 0), -1: one(ix < nx - 1)}
    yp, ym, zp, zm = one(iy < ny - 1), one(iy > 0), one(iz < nz - 1), one(iz > 0)

    def fetch(phase, f, mx, in_y, in_z):
        land = phases[phase][1]
        rows, lanes = (sub8, lane8) if in_y else (None, lane)
        if in_y:
            y_parts = [
                (m, jnp.where(sub8 < 4, yp if m != 1 else 0, ym if m != -1 else 0))
                for m in moves(ny)
            ]
        else:
            y_parts = [(0, None)]
        if in_z:
            z_parts = [
                (m, jnp.where(lanes % 2 == 0, zp if m != 1 else 0, zm if m != -1 else 0))
                for m in moves(nz)
            ]
        else:
            z_parts = [(0, None)]
        out = None
        for my, cy in y_parts:
            for mz, cz in z_parts:
                value = land[(mx, my, mz)][f]
                ok = has_x[mx] if mx else 1
                for c in (cy, cz):
                    if c is not None:
                        ok = c * ok
                keep = jnp.broadcast_to(ok, value.shape[-2:]) > 0
                if value.ndim == 3:
                    keep = keep[None]
                other = jnp.zeros_like(value) if out is None else out
                out = jnp.where(jnp.broadcast_to(keep, value.shape), value, other)
        return out

    def halo(phase, f):
        return dict(
            x={m: fetch(phase, f, m, False, False)[0] for m in (1, -1)},
            y=fetch(phase, f, 0, True, False),
            xy={m: fetch(phase, f, m, True, False)[0] for m in (1, -1)},
            z=fetch(phase, f, 0, False, True),
            xz={m: fetch(phase, f, m, False, True) for m in (1, -1)},
            yz=fetch(phase, f, 0, True, True),
        )

    def extend(u, parts):
        middle = jnp.concatenate([u, parts["y"]], axis=1)
        ends = {m: jnp.concatenate([parts["x"][m], parts["xy"][m]], axis=0) for m in (1, -1)}
        planes = [ends[1]] + [middle[p] for p in range(lx)] + [ends[-1]]
        z_rows = jnp.concatenate([parts["z"], parts["yz"]], axis=0)
        edges = (
            [roll(parts["xz"][1], -(2 * lx - 1), 1)]
            + [roll(z_rows, -(2 * p + 1), 1) for p in range(lx)]
            + [roll(parts["xz"][-1], -1, 1)]
        )
        return planes, edges

    def variant(ext, dy, dz, p):
        planes, edges = ext
        x = planes[p]
        outer = p in (0, lx + 1)
        if outer and dy and dz:
            return None
        if dz:
            rows = ly if dy == 0 else ly + 8
            at = lax.broadcasted_iota(jnp.int32, (rows, lz), 1)
            x = jnp.where(
                at == (lz - 1 if dz == 1 else 0), edges[p][:rows], roll(x[:rows], -dz, 1)
            )
        if dy:
            x = roll(x, -dy, 0)
        return x[:ly]

    def store_variants(ref, where, ext):
        for k, (dy, dz) in enumerate(VARIANTS):
            for p in range(lx + 2):
                x = variant(ext, dy, dz, p)
                if x is not None:
                    ref[where, k, p] = x

    def neighbour(ref, where, offset, p):
        return ref[where, VARIANTS.index(offset[1:]), p + 1 + offset[0]]

    for load in loads[:5]:
        load.wait()
    tissue = tissue_ref[...].astype(jnp.float32)
    factor = jnp.zeros(shape, jnp.float32)
    for label in range(regions):
        factor = jnp.where(region_ref[...] == label, cond_ref[label], factor)
    factor = tissue * factor
    sector = sector_ref[...].astype(jnp.float32)
    stage_fields(0, (factor, sector, v_ref[...]))
    pl.semaphore_wait(barrier, n - 1)
    send(0)
    for load in loads[5:]:
        load.wait()

    def fibres(codes):
        found = [jnp.zeros(codes.shape, jnp.float32) for _ in PAIR_OFFSETS]
        for label in range(sectors):
            same = codes == float(label)
            for d in range(len(PAIR_OFFSETS)):
                found[d] = jnp.where(same, table_ref[label, d], found[d])
        return found

    def ionic(volts, gate):
        s = 1.0 / (1.0 + jnp.exp(-(volts - gate_level) / gate_width))
        drive_v = gate * volts * volts * (1.0 - volts) / tau_inward - volts / tau_outward
        drive_h = (1.0 - s) * (1.0 - gate) / tau_opening - s * gate / tau_closing
        return drive_v, drive_h

    def partials(volts, gate):
        s = 1.0 / (1.0 + jnp.exp(-(volts - gate_level) / gate_width))
        slope = s * (1.0 - s) / gate_width
        vv = gate * (2.0 * volts - 3.0 * volts * volts) / tau_inward - 1.0 / tau_outward
        vh = volts * volts * (1.0 - volts) / tau_inward
        hv = slope * (-(1.0 - gate) / tau_opening - gate / tau_closing)
        hh = -(1.0 - s) / tau_opening - s / tau_closing
        return vv, vh, hv, hh

    def spread(ref, where, u, p):
        total = -diag[p] * u
        for o, (_, offset) in enumerate(OFFSETS):
            total = total + coef[o, p] * neighbour(ref, where, offset, p)
        return total

    fibre = fibres(sector)
    flux = [factor * f for f in fibre]
    volts, gate = v_ref[...], h_ref[...]
    drive_v, drive_h = ionic(volts, gate)

    receive(0)
    fac_halo = halo(0, 0)
    sec_halo = halo(0, 1)
    fac_ext = extend(factor, fac_halo)

    halo_flux = [dict() for _ in PAIR_OFFSETS]
    for name in fac_halo:
        entry, codes = fac_halo[name], sec_halo[name]
        if isinstance(entry, dict):
            for d in range(len(PAIR_OFFSETS)):
                halo_flux[d][name] = {}
            for m in entry:
                for d, f in enumerate(fibres(codes[m])):
                    halo_flux[d][name][m] = entry[m] * f
        else:
            for d, f in enumerate(fibres(codes)):
                halo_flux[d][name] = entry * f

    beside = {}
    for dy, dz in VARIANTS:
        beside[dy, dz] = [
            None if x is None else jnp.where(x > 0.0, 1.0, 0.0)
            for x in (variant(fac_ext, dy, dz, p) for p in range(lx + 2))
        ]
    for o, (d, offset) in enumerate(OFFSETS):
        dx, dy, dz = offset
        ext = extend(flux[d], halo_flux[d])
        for p in range(lx):
            near = beside[dy, dz][p + 1 + dx]
            c = 0.5 * (flux[d][p] * near + variant(ext, dy, dz, p + 1 + dx) * tissue[p])
            coef[o, p] = c
            diag[p] = c if o == 0 else diag[p] + c
            grad[o, p] = (-0.5 * tissue[p]) * near * fibre[d][p]

    volts_at, gate_at = [], []
    for step in range(WINDOW_STEPS):
        volts_at.append(volts)
        gate_at.append(gate)
        if step:
            stage_fields(step, (volts,))
            send(step)
            drive_v, drive_h = ionic(volts, gate)
        base = volts + tissue * (step_size * drive_v)
        gate = gate + tissue * (step_size * drive_h)
        if step:
            receive(step)
        store_variants(vvar, step, extend(volts, halo(step, 0 if step else 2)))
        volts = jnp.stack(
            [base[p] + tissue[p] * spread(vvar, step, volts[p], p) for p in range(lx)]
        )

    back_v = av_ref[...] + tissue * (volts - rec_ref[...])
    back_h = ah_ref[...]
    terms = jnp.zeros(shape, jnp.float32)

    def add_terms(terms, step, masked):
        rows = []
        for p in range(lx):
            total = terms[p]
            mid_m, mid_v = masked[p], volts_at[step][p]
            for o, (_, offset) in enumerate(OFFSETS):
                total = total + grad[o, p] * (
                    (neighbour(mvar, step, offset, p) - mid_m)
                    * (neighbour(vvar, step, offset, p) - mid_v)
                )
            rows.append(total)
        return jnp.stack(rows)

    pending = None
    phase = WINDOW_STEPS
    for step in reversed(range(WINDOW_STEPS)):
        masked = tissue * back_v
        stage_fields(phase, (masked,))
        send(phase)
        if pending is not None:
            terms = add_terms(terms, *pending)
        vv, vh, hv, hh = partials(volts_at[step], gate_at[step])
        base = back_v + step_size * tissue * (vv * back_v + hv * back_h)
        back_h = back_h + step_size * tissue * (vh * back_v + hh * back_h)
        receive(phase)
        store_variants(mvar, step, extend(masked, halo(phase, 0)))
        if step:
            back_v = jnp.stack(
                [base[p] + spread(mvar, step, masked[p], p) for p in range(lx)]
            )
        pending = (step, masked)
        phase += 1

    terms = add_terms(terms, *pending)
    row = lax.broadcasted_iota(jnp.int32, (8, lz), 0)
    column = lax.broadcasted_iota(jnp.int32, (1, lz), 1)
    sums = jnp.zeros((1, lz), jnp.float32)
    region = region_ref[...]
    for label in range(regions):
        own = jnp.sum(jnp.where(region == label, terms, 0.0), axis=(0, 1))[None]
        own = jnp.sum(own, axis=1, keepdims=True)
        sums = jnp.where(column == label, own, sums)
    gathered[me] = jnp.where(row == 0, jnp.broadcast_to(sums, (8, lz)), 0.0)

    def red_copy(rel, slot, target):
        return pltpu.make_async_remote_copy(
            src_ref=gathered.at[me],
            dst_ref=gathered.at[slot],
            send_sem=red_send.at[rel],
            recv_sem=red_recv.at[slot],
            device_id=target,
            device_id_type=MESH,
        )

    def red_start(rel, slot, target):
        red_copy(rel, me, target).start()

    def red_wait(rel, slot, target):
        red_copy(rel, slot, target).wait_recv()

    def red_finish(rel, slot, target):
        red_copy(rel, me, target).wait_send()

    each_other(red_start)
    for p in range(lx):
        final_v[p] = base[p] + spread(mvar, 0, masked[p], p)
    final_h[...] = back_h
    saves = [
        pltpu.make_async_copy(src, dst, save_sem.at[k])
        for k, (src, dst) in enumerate(((final_v, out_v), (final_h, out_h), (final_s, out_s)))
    ]
    saves[0].start()
    saves[1].start()
    for k in range(len(phase_fields)):
        finish_sends(k)
    each_other(red_wait)
    total = jnp.sum(gathered[...], axis=0)[0:1] * scale
    final_s[...] = jnp.broadcast_to(total, (8, lz))
    saves[2].start()
    each_other(red_finish)
    for save in saves:
        save.wait()


def hand_out(in_v, in_h, in_s, out_v, out_h, out_s, row, sem):
    copies = [
        pltpu.make_async_copy(src, dst, sem.at[k])
        for k, (src, dst) in enumerate(((in_s, row), (in_v, out_v), (in_h, out_h)))
    ]
    for copy in copies:
        copy.start()
    copies[0].wait()
    out_s[...] = row[0, : out_s.shape[0]]
    for copy in copies[1:]:
        copy.wait()


def local(*args):
    potential, fibre_table, conductance = args[0], args[8], args[9]
    counts = tuple(lax.axis_size(a) for a in ("gx", "gy", "gz"))
    nx, ny, nz = counts
    shape = potential.shape
    lx, ly, lz = shape
    regions, sectors = conductance.shape[0], fibre_table.shape[0]
    cells = lx * ly * lz * nx * ny * nz
    scale = gradient_gain / math.sqrt(cells / regions)
    phase_fields = (3,) + (1,) * (2 * WINDOW_STEPS - 1)
    f32 = jnp.float32
    pairs = len(OFFSETS)
    variants = len(VARIANTS)
    n = nx * ny * nz
    order = (7, 5, 9, 6, 0, 8, 1, 2, 3, 4)
    operands = [args[k] for k in order]
    scratch = [
        (pltpu.SMEM if k >= 8 else pltpu.VMEM)(args[k].shape, args[k].dtype) for k in order
    ]
    scratch += [
        pltpu.SemaphoreType.DMA((len(order),)),
        pltpu.VMEM(shape, f32),
        pltpu.VMEM(shape, f32),
        pltpu.VMEM((8, lz), f32),
        pltpu.SemaphoreType.DMA((3,)),
        pltpu.VMEM((pairs,) + shape, f32),
        pltpu.VMEM((pairs,) + shape, f32),
        pltpu.VMEM(shape, f32),
        pltpu.VMEM((WINDOW_STEPS, variants, lx + 2, ly, lz), f32),
        pltpu.VMEM((WINDOW_STEPS, variants, lx + 2, ly, lz), f32),
        pltpu.VMEM((n, 8, lz), f32),
        pltpu.SemaphoreType.DMA((n,)),
        pltpu.SemaphoreType.DMA((n,)),
    ]
    moved = messages(ny, nz)
    for fields in phase_fields:
        scratch += [
            pltpu.VMEM((fields, 2, ly, lz), f32),
            pltpu.VMEM((fields, lx, 8, lz), f32),
            pltpu.VMEM((fields, ly, lz), f32),
            pltpu.VMEM((fields, 8, lz), f32),
        ]
        scratch += [pltpu.VMEM(land_shape(move, fields, shape), f32) for move in moved]
        scratch += [pltpu.SemaphoreType.DMA((len(moved),))] * 2
    vmem = pl.BlockSpec(memory_space=pltpu.VMEM)
    hbm = pl.BlockSpec(memory_space=pltpu.HBM)
    back_v, back_h, totals = pl.pallas_call(
        functools.partial(kernel, counts, phase_fields, regions, sectors, scale),
        out_shape=(
            jax.ShapeDtypeStruct(shape, f32),
            jax.ShapeDtypeStruct(shape, f32),
            jax.ShapeDtypeStruct((8, lz), f32),
        ),
        in_specs=[hbm] * len(order),
        out_specs=(hbm, hbm, hbm),
        scratch_shapes=scratch,
        compiler_params=pltpu.CompilerParams(
            collective_id=0, has_side_effects=True, vmem_limit_bytes=63 * 2**20
        ),
        name="adjoint_window",
    )(*operands)
    return pl.pallas_call(
        hand_out,
        out_shape=(
            jax.ShapeDtypeStruct(shape, f32),
            jax.ShapeDtypeStruct(shape, f32),
            jax.ShapeDtypeStruct((regions,), f32),
        ),
        in_specs=[hbm] * 3,
        out_specs=(hbm, hbm, vmem),
        scratch_shapes=[pltpu.VMEM((8, lz), f32), pltpu.SemaphoreType.DMA((3,))],
        compiler_params=pltpu.CompilerParams(vmem_limit_bytes=63 * 2**20),
        name="hand_out",
    )(back_v, back_h, totals)


def solution(mesh):
    block = P(("twin", "gx"), "gy", "gz")
    in_specs = (block,) * 8 + (P("twin", None), P("twin"))
    out_specs = (block, block, P("twin"))
    return jax.shard_map(local, mesh=mesh, in_specs=in_specs, out_specs=out_specs, check_vma=False)
```

```python
import functools
import math

import jax
import jax.numpy as jnp
from jax import lax
from jax.experimental import pallas as pl
from jax.experimental.pallas import tpu as pltpu
from jax.sharding import PartitionSpec as P

WINDOW_STEPS = 3

step_size = 0.1
tau_inward = 0.3
tau_outward = 6.0
tau_opening = 12.0
tau_closing = 15.0
gate_level = 0.13
gate_width = 0.02
gradient_gain = 30.0
PAIR_OFFSETS = (
    (1, 0, 0),
    (0, 1, 0),
    (0, 0, 1),
    (1, 1, 0),
    (1, -1, 0),
    (1, 0, 1),
    (1, 0, -1),
    (0, 1, 1),
    (0, 1, -1),
)
OFFSETS = tuple(
    (d, tuple(sign * part for part in base))
    for d, base in enumerate(PAIR_OFFSETS)
    for sign in (1, -1)
)
VARIANTS = tuple((dy, dz) for dy in (0, 1, -1) for dz in (0, 1, -1))
FLIP = 2
MESH = pl.DeviceIdType.MESH


def moves(size):
    if size == 1:
        return ()
    return (FLIP,) if size == 2 else (1, -1)


def messages(ny, nz):
    found = []
    for mx in (0, 1, -1):
        for my in (0,) + moves(ny):
            for mz in (0,) + moves(nz):
                if 1 <= (mx != 0) + (my != 0) + (mz != 0) <= 2:
                    found.append((mx, my, mz))
    return sorted(found, key=lambda m: (m[0] == 0, m[2] == 0, m[1] == 0))


def land_shape(move, fields, shape):
    lx, ly, lz = shape
    mx, my, mz = move
    if mz:
        return (fields, 8 if my else ly, lz)
    return (fields, 1 if mx else lx, 8 if my else ly, lz)


def kernel(
    counts,
    phase_fields,
    regions,
    sectors,
    scale,
    *refs,
):
    inputs, refs = refs[:10], refs[10:]
    out_v, out_h, out_s = refs[:3]
    held, (load_sem, *refs) = refs[3:13], refs[13:]
    loads = [
        pltpu.make_async_copy(src, dst, load_sem.at[k])
        for k, (src, dst) in enumerate(zip(inputs, held))
    ]
    for load in loads:
        load.start()
    (region_ref, tissue_ref, cond_ref, sector_ref, v_ref, table_ref, h_ref, av_ref, ah_ref, rec_ref) = held
    (final_v, final_h, save_sem, *refs) = refs
    (coef, grad, diag, vvar, mvar, gathered, red_send, red_recv, *rest) = refs
    nx, ny, nz = counts
    shape = v_ref.shape
    lx, ly, lz = shape
    moved = messages(ny, nz)
    phases = []
    for _ in phase_fields:
        stage = [rest.pop(0) for _ in range(4)]
        land = {move: rest.pop(0) for move in moved}
        phases.append((stage, land, rest.pop(0), rest.pop(0)))

    ix, iy, iz = lax.axis_index("gx"), lax.axis_index("gy"), lax.axis_index("gz")
    n = nx * ny * nz
    me = (ix * ny + iy) * nz + iz

    def device(index):
        return {"gx": index // (ny * nz), "gy": (index // nz) % ny, "gz": index % nz}

    barrier = pltpu.get_barrier_semaphore()

    def wrapped(index, count, by):
        if by == 0:
            return index
        moved_on = index + by
        return jnp.where(moved_on >= count, moved_on - count, moved_on)

    def greet(rel, slot, target):
        pl.semaphore_signal(barrier, inc=1, device_id=target, device_id_type=MESH)

    def each_other(body):
        if n <= 64:
            for rel in range(n - 1, 0, -1):
                tx = wrapped(ix, nx, rel // (ny * nz))
                ty = wrapped(iy, ny, rel // nz % ny)
                tz = wrapped(iz, nz, rel % nz)
                body(rel, (tx * ny + ty) * nz + tz, {"gx": tx, "gy": ty, "gz": tz})
        else:

            def step(rel, carry):
                slot = (me + rel) % n
                body(rel, slot, device(slot))
                return carry

            lax.fori_loop(1, n, step, 0)

    each_other(greet)

    def along(index, count, move):
        if move == 0:
            return index, None
        if move == FLIP:
            return 1 - index, None
        return index + move, (index < count - 1) if move == 1 else (index > 0)

    def both(conds):
        conds = [c for c in conds if c is not None]
        if not conds:
            return None
        out = conds[0]
        for c in conds[1:]:
            out = jnp.logical_and(out, c)
        return out

    def guarded(cond, body):
        if cond is None:
            body()
        else:
            pl.when(cond)(body)

    def copy_of(phase, k):
        (sx, sy, sz, syz), land, send, recv = phases[phase]
        mx, my, mz = move = moved[k]
        tx, cx = along(ix, nx, mx)
        ty, cy = along(iy, ny, my)
        tz, cz = along(iz, nz, mz)
        back = [along(i, c, m if m == FLIP else -m)[1] for i, c, m in
                ((ix, nx, mx), (iy, ny, my), (iz, nz, mz))]
        if mz:
            src = syz if my else sz
        elif my:
            src = sy
            if mx:
                src = sy.at[:, pl.ds(lx - 1 if mx == 1 else 0, 1)]
        else:
            src = sx.at[:, pl.ds(1 if mx == 1 else 0, 1)]
        copy = pltpu.make_async_remote_copy(
            src_ref=src,
            dst_ref=land[move],
            send_sem=send.at[k],
            recv_sem=recv.at[k],
            device_id={"gx": tx, "gy": ty, "gz": tz},
            device_id_type=MESH,
        )
        return copy, both((cx, cy, cz)), both(back)

    lane3 = lax.broadcasted_iota(jnp.int32, (1, 1, lz), 2)
    sub8 = lax.broadcasted_iota(jnp.int32, (8, lz), 0)
    lane = lax.broadcasted_iota(jnp.int32, (ly, lz), 1)
    lane8 = lax.broadcasted_iota(jnp.int32, (8, lz), 1)

    def roll(x, shift, axis):
        size = x.shape[axis]
        shift = shift % size
        return x if shift == 0 else pltpu.roll(x, shift, axis)

    def stage_fields(phase, fields):
        sx, sy, sz, syz = phases[phase][0]
        for f, u in enumerate(fields):
            sx[f, 0] = u[0]
            sx[f, 1] = u[lx - 1]
            sy[f] = jnp.where((sub8 < 4)[None], u[:, :8], u[:, ly - 8 :])
            packed = jnp.zeros((ly, lz), jnp.float32)
            for p in range(lx):
                edge = jnp.where(lane == 0, roll(u[p], 1, 1), roll(u[p], -1, 1))
                here = (lane == 2 * p) | (lane == 2 * p + 1)
                packed = jnp.where(here, roll(edge, 2 * p + 1, 1), packed)
            sz[f] = packed
            syz[f] = jnp.where(sub8 < 4, packed[:8], packed[ly - 8 :])

    def send(phase):
        for k in range(len(moved)):
            copy, cond, _ = copy_of(phase, k)
            guarded(cond, copy.start)

    def receive(phase):
        for k in range(len(moved)):
            copy, _, cond = copy_of(phase, k)
            guarded(cond, copy.wait_recv)

    def finish_sends(phase):
        for k in range(len(moved)):
            copy, cond, _ = copy_of(phase, k)
            guarded(cond, copy.wait_send)

    one = lambda cond: jnp.where(cond, 1, 0)
    has_x = {1: one(ix > 0), -1: one(ix < nx - 1)}
    yp, ym, zp, zm = one(iy < ny - 1), one(iy > 0), one(iz < nz - 1), one(iz > 0)

    def fetch(phase, f, mx, in_y, in_z):
        land = phases[phase][1]
        rows, lanes = (sub8, lane8) if in_y else (None, lane)
        if in_y:
            y_parts = [
                (m, jnp.where(sub8 < 4, yp if m != 1 else 0, ym if m != -1 else 0))
                for m in moves(ny)
            ]
        else:
            y_parts = [(0, None)]
        if in_z:
            z_parts = [
                (m, jnp.where(lanes % 2 == 0, zp if m != 1 else 0, zm if m != -1 else 0))
                for m in moves(nz)
            ]
        else:
            z_parts = [(0, None)]
        out = None
        for my, cy in y_parts:
            for mz, cz in z_parts:
                value = land[(mx, my, mz)][f]
                ok = has_x[mx] if mx else 1
                for c in (cy, cz):
                    if c is not None:
                        ok = c * ok
                keep = jnp.broadcast_to(ok, value.shape[-2:]) > 0
                if value.ndim == 3:
                    keep = keep[None]
                other = jnp.zeros_like(value) if out is None else out
                out = jnp.where(jnp.broadcast_to(keep, value.shape), value, other)
        return out

    def halo(phase, f):
        return dict(
            x={m: fetch(phase, f, m, False, False)[0] for m in (1, -1)},
            y=fetch(phase, f, 0, True, False),
            xy={m: fetch(phase, f, m, True, False)[0] for m in (1, -1)},
            z=fetch(phase, f, 0, False, True),
            xz={m: fetch(phase, f, m, False, True) for m in (1, -1)},
            yz=fetch(phase, f, 0, True, True),
        )

    def lane_shifts(u):
        return {dz: [roll(u[p], -dz, 1) for p in range(lx)] for dz in (1, -1)}

    def extend(u, parts, shifts=None):
        middle = jnp.concatenate([u, parts["y"]], axis=1)
        ends = {m: jnp.concatenate([parts["x"][m], parts["xy"][m]], axis=0) for m in (1, -1)}
        planes = [ends[1]] + [middle[p] for p in range(lx)] + [ends[-1]]
        z_rows = jnp.concatenate([parts["z"], parts["yz"]], axis=0)
        edges = (
            [roll(parts["xz"][1], -(2 * lx - 1), 1)]
            + [roll(z_rows, -(2 * p + 1), 1) for p in range(lx)]
            + [roll(parts["xz"][-1], -1, 1)]
        )
        return planes, edges, shifts

    def variant(ext, dy, dz, p):
        planes, edges, shifts = ext
        x = planes[p]
        outer = p in (0, lx + 1)
        if outer and dy and dz:
            return None
        if dz:
            rows = ly if dy == 0 else ly + 8
            at = lax.broadcasted_iota(jnp.int32, (rows, lz), 1)
            if shifts is None or outer:
                along_lanes = roll(x[:rows], -dz, 1)
            else:
                along_lanes = shifts[dz][p - 1]
                if dy:
                    along_lanes = jnp.concatenate([along_lanes, roll(x[ly:], -dz, 1)], axis=0)
            x = jnp.where(at == (lz - 1 if dz == 1 else 0), edges[p][:rows], along_lanes)
        if dy:
            x = roll(x, -dy, 0)
        return x[:ly]

    def store_variants(ref, where, ext):
        for k, (dy, dz) in enumerate(VARIANTS):
            for p in range(lx + 2):
                x = variant(ext, dy, dz, p)
                if x is not None:
                    ref[where, k, p] = x

    def neighbour(ref, where, offset, p):
        return ref[where, VARIANTS.index(offset[1:]), p + 1 + offset[0]]

    for load in loads[:5]:
        load.wait()
    tissue = tissue_ref[...].astype(jnp.float32)
    factor = jnp.zeros(shape, jnp.float32)
    for label in range(regions):
        factor = jnp.where(region_ref[...] == label, cond_ref[label], factor)
    factor = tissue * factor
    sector = sector_ref[...].astype(jnp.float32)
    stage_fields(0, (factor, sector, v_ref[...]))
    pl.semaphore_wait(barrier, n - 1)
    send(0)
    for load in loads[5:]:
        load.wait()

    def fibres(codes):
        found = [jnp.zeros(codes.shape, jnp.float32) for _ in PAIR_OFFSETS]
        for label in range(sectors):
            same = codes == float(label)
            for d in range(len(PAIR_OFFSETS)):
                found[d] = jnp.where(same, table_ref[label, d], found[d])
        return found

    def ionic(volts, gate):
        s = 1.0 / (1.0 + jnp.exp(-(volts - gate_level) / gate_width))
        drive_v = gate * volts * volts * (1.0 - volts) / tau_inward - volts / tau_outward
        drive_h = (1.0 - s) * (1.0 - gate) / tau_opening - s * gate / tau_closing
        return drive_v, drive_h

    def partials(volts, gate):
        s = 1.0 / (1.0 + jnp.exp(-(volts - gate_level) / gate_width))
        slope = s * (1.0 - s) / gate_width
        vv = gate * (2.0 * volts - 3.0 * volts * volts) / tau_inward - 1.0 / tau_outward
        vh = volts * volts * (1.0 - volts) / tau_inward
        hv = slope * (-(1.0 - gate) / tau_opening - gate / tau_closing)
        hh = -(1.0 - s) / tau_opening - s / tau_closing
        return vv, vh, hv, hh

    def spread(ref, where, u, p):
        total = -diag[p] * u
        for o, (_, offset) in enumerate(OFFSETS):
            total = total + coef[o, p] * neighbour(ref, where, offset, p)
        return total

    fibre = fibres(sector)
    flux = [factor * f for f in fibre]
    volts, gate = v_ref[...], h_ref[...]
    drive_v, drive_h = ionic(volts, gate)

    shifts = lane_shifts(volts)
    fac_shifts = lane_shifts(factor)
    flux_shifts = [
        lane_shifts(f) if base[2] else None for f, base in zip(flux, PAIR_OFFSETS)
    ]

    receive(0)
    fac_halo = halo(0, 0)
    sec_halo = halo(0, 1)
    fac_ext = extend(factor, fac_halo, fac_shifts)

    halo_flux = [dict() for _ in PAIR_OFFSETS]
    for name in fac_halo:
        entry, codes = fac_halo[name], sec_halo[name]
        if isinstance(entry, dict):
            for d in range(len(PAIR_OFFSETS)):
                halo_flux[d][name] = {}
            for m in entry:
                for d, f in enumerate(fibres(codes[m])):
                    halo_flux[d][name][m] = entry[m] * f
        else:
            for d, f in enumerate(fibres(codes)):
                halo_flux[d][name] = entry * f

    beside = {}
    for dy, dz in VARIANTS:
        beside[dy, dz] = [
            None if x is None else jnp.where(x > 0.0, 1.0, 0.0)
            for x in (variant(fac_ext, dy, dz, p) for p in range(lx + 2))
        ]
    for o, (d, offset) in enumerate(OFFSETS):
        dx, dy, dz = offset
        ext = extend(flux[d], halo_flux[d], flux_shifts[d])
        for p in range(lx):
            near = beside[dy, dz][p + 1 + dx]
            c = 0.5 * (flux[d][p] * near + variant(ext, dy, dz, p + 1 + dx) * tissue[p])
            coef[o, p] = c
            diag[p] = c if o == 0 else diag[p] + c

    def store_grad():
        for o, (d, (dx, dy, dz)) in enumerate(OFFSETS):
            for p in range(lx):
                near = beside[dy, dz][p + 1 + dx]
                grad[o, p] = (-0.5 * tissue[p]) * near * fibre[d][p]

    volts_at, gate_at = [], []
    for step in range(WINDOW_STEPS):
        volts_at.append(volts)
        gate_at.append(gate)
        if step:
            stage_fields(step, (volts,))
            send(step)
            if step == 1:
                store_grad()
            drive_v, drive_h = ionic(volts, gate)
        base = volts + tissue * (step_size * drive_v)
        gate = gate + tissue * (step_size * drive_h)
        if step:
            shifts = lane_shifts(volts)
            receive(step)
        store_variants(vvar, step, extend(volts, halo(step, 0 if step else 2), shifts))
        volts = jnp.stack(
            [base[p] + tissue[p] * spread(vvar, step, volts[p], p) for p in range(lx)]
        )

    back_v = av_ref[...] + tissue * (volts - rec_ref[...])
    back_h = ah_ref[...]
    terms = jnp.zeros(shape, jnp.float32)

    def add_terms(terms, step, masked):
        rows = []
        for p in range(lx):
            total = terms[p]
            mid_m, mid_v = masked[p], volts_at[step][p]
            for o, (_, offset) in enumerate(OFFSETS):
                total = total + grad[o, p] * (
                    (neighbour(mvar, step, offset, p) - mid_m)
                    * (neighbour(vvar, step, offset, p) - mid_v)
                )
            rows.append(total)
        return jnp.stack(rows)

    pending = None
    phase = WINDOW_STEPS
    for step in reversed(range(WINDOW_STEPS)):
        masked = tissue * back_v
        stage_fields(phase, (masked,))
        send(phase)
        if pending is not None:
            terms = add_terms(terms, *pending)
        vv, vh, hv, hh = partials(volts_at[step], gate_at[step])
        base = back_v + step_size * tissue * (vv * back_v + hv * back_h)
        back_h = back_h + step_size * tissue * (vh * back_v + hh * back_h)
        shifts = lane_shifts(masked)
        receive(phase)
        store_variants(mvar, step, extend(masked, halo(phase, 0), shifts))
        if step:
            back_v = jnp.stack(
                [base[p] + spread(mvar, step, masked[p], p) for p in range(lx)]
            )
        pending = (step, masked)
        phase += 1

    terms = add_terms(terms, *pending)
    row = lax.broadcasted_iota(jnp.int32, (8, lz), 0)
    column = lax.broadcasted_iota(jnp.int32, (1, lz), 1)
    sums = jnp.zeros((1, lz), jnp.float32)
    region = region_ref[...]
    for label in range(regions):
        own = jnp.sum(jnp.where(region == label, terms, 0.0), axis=(0, 1))[None]
        own = jnp.sum(own, axis=1, keepdims=True)
        sums = jnp.where(column == label, own, sums)
    gathered[me] = jnp.where(row == 0, jnp.broadcast_to(sums, (8, lz)), 0.0)

    def red_copy(rel, slot, target):
        return pltpu.make_async_remote_copy(
            src_ref=gathered.at[me],
            dst_ref=gathered.at[slot],
            send_sem=red_send.at[rel],
            recv_sem=red_recv.at[slot],
            device_id=target,
            device_id_type=MESH,
        )

    def red_start(rel, slot, target):
        red_copy(rel, me, target).start()

    def red_wait(rel, slot, target):
        red_copy(rel, slot, target).wait_recv()

    def red_finish(rel, slot, target):
        red_copy(rel, me, target).wait_send()

    each_other(red_start)
    for p in range(lx):
        final_v[p] = base[p] + spread(mvar, 0, masked[p], p)
    final_h[...] = back_h
    saves = [
        pltpu.make_async_copy(src, dst, save_sem.at[k])
        for k, (src, dst) in enumerate(((final_v, out_v), (final_h, out_h)))
    ]
    saves[0].start()
    saves[1].start()
    for k in range(len(phase_fields)):
        finish_sends(k)
    each_other(red_wait)
    total = jnp.sum(gathered[...], axis=0)[0:1] * scale
    out_s[...] = total[0, :regions]
    each_other(red_finish)
    for save in saves:
        save.wait()


def local(*args):
    potential, fibre_table, conductance = args[0], args[8], args[9]
    counts = tuple(lax.axis_size(a) for a in ("gx", "gy", "gz"))
    nx, ny, nz = counts
    shape = potential.shape
    lx, ly, lz = shape
    regions, sectors = conductance.shape[0], fibre_table.shape[0]
    cells = lx * ly * lz * nx * ny * nz
    scale = gradient_gain / math.sqrt(cells / regions)
    phase_fields = (3,) + (1,) * (2 * WINDOW_STEPS - 1)
    f32 = jnp.float32
    pairs = len(OFFSETS)
    variants = len(VARIANTS)
    n = nx * ny * nz
    order = (7, 5, 9, 6, 0, 8, 1, 2, 3, 4)
    operands = [args[k] for k in order]
    scratch = [
        (pltpu.SMEM if k >= 8 else pltpu.VMEM)(args[k].shape, args[k].dtype) for k in order
    ]
    scratch += [
        pltpu.SemaphoreType.DMA((len(order),)),
        pltpu.VMEM(shape, f32),
        pltpu.VMEM(shape, f32),
        pltpu.SemaphoreType.DMA((2,)),
        pltpu.VMEM((pairs,) + shape, f32),
        pltpu.VMEM((pairs,) + shape, f32),
        pltpu.VMEM(shape, f32),
        pltpu.VMEM((WINDOW_STEPS, variants, lx + 2, ly, lz), f32),
        pltpu.VMEM((WINDOW_STEPS, variants, lx + 2, ly, lz), f32),
        pltpu.VMEM((n, 8, lz), f32),
        pltpu.SemaphoreType.DMA((n,)),
        pltpu.SemaphoreType.DMA((n,)),
    ]
    moved = messages(ny, nz)
    for fields in phase_fields:
        scratch += [
            pltpu.VMEM((fields, 2, ly, lz), f32),
            pltpu.VMEM((fields, lx, 8, lz), f32),
            pltpu.VMEM((fields, ly, lz), f32),
            pltpu.VMEM((fields, 8, lz), f32),
        ]
        scratch += [pltpu.VMEM(land_shape(move, fields, shape), f32) for move in moved]
        scratch += [pltpu.SemaphoreType.DMA((len(moved),))] * 2
    vmem = pl.BlockSpec(memory_space=pltpu.VMEM)
    hbm = pl.BlockSpec(memory_space=pltpu.HBM)
    return pl.pallas_call(
        functools.partial(kernel, counts, phase_fields, regions, sectors, scale),
        out_shape=(
            jax.ShapeDtypeStruct(shape, f32),
            jax.ShapeDtypeStruct(shape, f32),
            jax.ShapeDtypeStruct((regions,), f32),
        ),
        in_specs=[hbm] * len(order),
        out_specs=(hbm, hbm, vmem),
        scratch_shapes=scratch,
        compiler_params=pltpu.CompilerParams(
            collective_id=0, has_side_effects=True, vmem_limit_bytes=63 * 2**20
        ),
        name="adjoint_window",
    )(*operands)


def solution(mesh):
    block = P(("twin", "gx"), "gy", "gz")
    in_specs = (block,) * 8 + (P("twin", None), P("twin"))
    out_specs = (block, block, P("twin"))
    return jax.shard_map(local, mesh=mesh, in_specs=in_specs, out_specs=out_specs, check_vma=False)
```
